256 devices in a mesh: slab: 64 (over z, x, core), comp: 4 (over y).
Axes of the slice: x: 4, y: 4, z: 8, core: 2. Of those that a mesh axis runs over, the one named last changes fastest.
Arguments:
- kspace: bfloat16 [12, 4, 128, 16384], P('comp', None, None, 'slab'), may hold values from -4 to 4, as said below
- sensitivities: float32 [4, 128, 16384], P(None, 'slab'), may hold values from -2.5 to 2.5, as said below
- sampling: int32 [12, 128, 8192], P('comp', None, 'slab'), may hold values from 0 to 1, as said below
Outputs:
- coefficients: float32 [12, 128, 16384], P('comp', 'slab')
- residual: float32 [12, 128, 16384], P('comp', 'slab')
The draws below stay inside these ranges and needn't reach their ends.
Inputs may be any that keep to these rules, and one draw needn't show every extreme that they name: `sampling`: sampled (1) or not (0) for each component and k-space point. `sensitivities`: real and imaginary parts of each coil's sensitivity. `kspace`: real and imaginary parts of the projected data.
All inputs are finite; a program needn't handle non-finite values.
Results may differ from the reference program's by a relative error of at most 0.025.
Values may be sent and summed in bfloat16 or wider, within the bound.
No kernel may reach another device: no remote copies, remote signals or barrier semaphores. Data moves between devices by JAX's collectives and lax.ppermute only.
A program may use at most 128 MiB of HBM per device.

```python
import math
import jax
import jax.numpy as jnp
from jax import lax

NX = 128
NY = 128
NZ = 64
COILS = 4
COMPS = 12
ITERS = 2


def draw_sensitivities(key, part):
    key = jax.random.fold_in(key, 21)
    array_shape = (COILS, NX, NY * 2 * NZ)
    profile = jnp.sqrt(1.0 + 2.0 * jnp.arange(NX, dtype=jnp.float32) / (NX - 1))[None, :, None]
    noise_part = jnp.clip(jax.random.normal(key, array_shape, jnp.float32), -4.0, 4.0)
    return 0.35 * noise_part * profile


def draw_kspace(key, part):
    key = jax.random.fold_in(key, 37)
    array_shape = (COMPS, COILS, NX, NY * 2 * NZ)
    levels = 10.0 ** (-jnp.arange(COMPS, dtype=jnp.float32) / (COMPS - 1))
    noise_part = jnp.clip(jax.random.normal(key, array_shape, jnp.float32), -4.0, 4.0)
    return (noise_part * levels[:, None, None, None]).astype(jnp.bfloat16)


def draw_sampling(key, part):
    key = jax.random.fold_in(key, 53)
    ranks = jnp.arange(COMPS, dtype=jnp.int32)
    jitter = jax.random.randint(jax.random.fold_in(key, 7), (COMPS,), -500, 500, jnp.int32)
    thresholds = 3000 + 6000 * ranks // (COMPS - 1) + jitter
    tickets = jax.random.randint(key, (COMPS, NX, NY * NZ), 0, 10000, jnp.int32)
    return (tickets < thresholds[:, None, None]).astype(jnp.int32)


def setup_inputs(seed: int = 0) -> dict:
    key_list = jax.random.split(jax.random.key(seed), 4)
    kspace = draw_kspace(jax.random.fold_in(key_list[3], 71), 0)
    sensitivities = draw_sensitivities(jax.random.fold_in(key_list[3], 71), 0)
    sampling = draw_sampling(jax.random.fold_in(key_list[3], 71), 0)
    return {"kspace": kspace, "sensitivities": sensitivities, "sampling": sampling}


def fourier_blocks(length, orientation):
    positions = jnp.arange(length, dtype=jnp.int32)
    angles = (positions[:, None] * positions[None, :] % length).astype(jnp.float32) * (2.0 * math.pi / length)
    scaling = 1.0 / math.sqrt(length)
    real_part = jnp.cos(angles) * scaling
    imaginary = orientation * jnp.sin(angles) * scaling
    top_rows = jnp.stack([real_part, -imaginary], 1)
    low_rows = jnp.stack([imaginary, real_part], 1)
    return jnp.stack([top_rows, low_rows], 0).astype(jnp.bfloat16)

def make_tables(orientation):
    last_matrix = fourier_blocks(NZ, orientation).reshape(2 * NZ, 2 * NZ).T
    middle_matrix = fourier_blocks(NY, orientation).transpose(1, 0, 3, 2).reshape(2 * NY, 2 * NY)
    first_blocks = fourier_blocks(NX, orientation)
    return (last_matrix, middle_matrix, first_blocks)

def along_last(values, last_matrix):
    shaped = values.reshape(values.shape[:-1] + (-1, last_matrix.shape[0])).astype(jnp.float32)
    result = jnp.einsum('...q,qp->...p', shaped, last_matrix.astype(jnp.float32), precision=lax.Precision.HIGHEST)
    return result.reshape(values.shape)

def along_middle(values, middle_matrix):
    shaped = values.reshape(values.shape[:-1] + (middle_matrix.shape[0], -1)).astype(jnp.float32)
    result = jnp.einsum('pq,...qz->...pz', middle_matrix.astype(jnp.float32), shaped, precision=lax.Precision.HIGHEST)
    return result.reshape(values.shape)

def along_first(values, first_blocks):
    shaped = values.reshape(values.shape[:-1] + (-1, 2, NZ)).astype(jnp.float32)
    result = jnp.einsum('akbx,...xybz->...kyaz', first_blocks.astype(jnp.float32), shaped, precision=lax.Precision.HIGHEST)
    return result.reshape(values.shape)

def spread(component_maps, coil_maps):
    field_view = component_maps.reshape(component_maps.shape[:-1] + (-1, 2, NZ))
    coil_view = coil_maps.reshape(coil_maps.shape[:-1] + (-1, 2, NZ))
    real_part = coil_view[..., 0, :] * field_view[..., 0, :] - coil_view[..., 1, :] * field_view[..., 1, :]
    imaginary = coil_view[..., 0, :] * field_view[..., 1, :] + coil_view[..., 1, :] * field_view[..., 0, :]
    result = jnp.stack([real_part, imaginary], -2)
    return result.reshape(result.shape[:-3] + (-1,))

def unspread(images, coil_maps):
    image_view = images.reshape(images.shape[:-1] + (-1, 2, NZ))
    coil_view = coil_maps.reshape(coil_maps.shape[:-1] + (-1, 2, NZ))
    real_part = coil_view[..., 0, :] * image_view[..., 0, :] + coil_view[..., 1, :] * image_view[..., 1, :]
    imaginary = coil_view[..., 0, :] * image_view[..., 1, :] - coil_view[..., 1, :] * image_view[..., 0, :]
    result = jnp.stack([real_part, imaginary], -2)
    return result.reshape(result.shape[:-3] + (-1,))

def pattern_grid(pattern):
    rows = pattern.astype(jnp.float32).reshape(pattern.shape[0], -1, 1, NZ)
    return jnp.broadcast_to(rows, rows.shape[:2] + (2, NZ)).reshape(pattern.shape[0], -1)

def adjoint_tail(masked, sensitivities, inverse):
    section_one = along_first(masked, inverse[2]).astype(jnp.bfloat16)
    section_two = along_middle(section_one, inverse[1]).astype(jnp.bfloat16)
    section_three = along_last(section_two, inverse[0])
    return lax.optimization_barrier(jnp.sum(unspread(section_three, sensitivities), axis=0))

def reference(kspace, sensitivities, sampling):
    forward = make_tables(-1.0)
    inverse = make_tables(1.0)

    def right_one(operands):
        samples, pattern = operands
        masked = (samples.astype(jnp.float32) * pattern_grid(pattern)[None]).astype(jnp.bfloat16)
        return adjoint_tail(masked, sensitivities, inverse)

    def normal_one(operands):
        estimate, pattern = operands
        images = spread(estimate[None], sensitivities).astype(jnp.bfloat16)
        section_one = along_last(images, forward[0]).astype(jnp.bfloat16)
        section_two = along_middle(section_one, forward[1]).astype(jnp.bfloat16)
        spectrum = along_first(section_two, forward[2])
        masked = (spectrum * pattern_grid(pattern)[None]).astype(jnp.bfloat16)
        return adjoint_tail(masked, sensitivities, inverse)
    right_side = lax.map(right_one, (kspace, sampling))
    coefficients = jnp.zeros_like(right_side)
    residual = right_side
    direction = right_side
    norm_now = jnp.sum(residual * residual)
    for iteration in range(ITERS):
        applied = lax.map(normal_one, (direction, sampling))
        step_size = norm_now / jnp.sum(direction * applied)
        coefficients = coefficients + step_size * direction
        residual = residual - step_size * applied
        if iteration + 1 < ITERS:
            norm_next = jnp.sum(residual * residual)
            direction = residual + norm_next / norm_now * direction
            norm_now = norm_next
    return (coefficients, residual)
```

```python
import functools
import math

import jax
import jax.numpy as jnp
import numpy as np
from jax import lax
from jax.experimental import pallas as pl
from jax.experimental.pallas import tpu as pltpu
from jax.sharding import PartitionSpec as P

NX = 128
NY = 128
NZ = 64
COILS = 4
PAIRS = COILS // 2
LANES = 2 * NZ
CHUNK = 3


def fourier_blocks(length, orientation):
    positions = np.arange(length)
    angles = (positions[:, None] * positions[None, :] % length) * (2.0 * math.pi / length)
    scaling = 1.0 / math.sqrt(length)
    real_part = np.cos(angles) * scaling
    imaginary = orientation * np.sin(angles) * scaling
    top_rows = np.stack([real_part, -imaginary], 1)
    low_rows = np.stack([imaginary, real_part], 1)
    return np.stack([top_rows, low_rows], 0).astype(np.float32)


def table(spec, *factors, shape):
    return np.einsum(spec, *factors).reshape(shape).astype(jnp.bfloat16)


def make_tables():
    two = np.eye(2, dtype=np.float32)
    slabs = NX // 2
    zf, zi = fourier_blocks(NZ, -1.0), fourier_blocks(NZ, 1.0)
    yf, yi = fourier_blocks(NY, -1.0), fourier_blocks(NY, 1.0)
    xf = fourier_blocks(NX, -1.0).reshape(2, NX, 2, slabs, 2)
    xi = fourier_blocks(NX, 1.0).reshape(2, slabs, 2, 2, NX)
    return {
        "zf": table("akbj,cd->cbjadk", zf, two, shape=(4 * NZ, 4 * NZ)),
        "zi": table("akbj,cd->bcjdak", zi, two, shape=(4 * NZ, 4 * NZ)),
        "yf": table("akbj,cd->kcabjd", yf, two, shape=(4 * NY, 4 * NY)),
        "yi": table("akbj,cd->akcjdb", yi, two, shape=(4 * NY, 4 * NY)),
        "xf": table("akbst,cd->caksdtb", xf, two, shape=(4 * NX, 4 * NX)),
        "xi": table("astbk,cd->sctadbk", xi, two, shape=(4 * NX, 4 * NX)),
        "order": table(
            "ab,cd,ef,gh->acegdfbh",
            two,
            two,
            two,
            np.eye(NZ, dtype=np.float32),
            shape=(8 * NZ, 8 * NZ),
        ),
    }


def product(left, right):
    return jnp.dot(left, right, preferred_element_type=jnp.float32)


def swap_halves(values):
    return pltpu.roll(values, NZ, values.ndim - 1)


def low_half(shape):
    return lax.broadcasted_iota(jnp.int32, shape, len(shape) - 1) < NZ


def masks_of(sampling):
    pattern = sampling.astype(jnp.float32)
    other = swap_halves(pattern)
    low = low_half(pattern.shape)
    return jnp.where(low, pattern, other), jnp.where(low, other, pattern)


def coil_factors(maps):
    other = swap_halves(maps)
    low = low_half(maps.shape)
    return jnp.where(low, maps, other), jnp.where(low, -other, maps)


def kspace_back(masked, xi):
    return product(xi, masked).astype(jnp.bfloat16)


def first_step(kspace, sampling, order, xi):
    columns = []
    for comp in range(kspace.shape[0]):
        masks = masks_of(sampling[comp])
        for pair in range(PAIRS):
            both = jnp.concatenate([kspace[comp, 2 * pair], kspace[comp, 2 * pair + 1]], 1)
            ordered = product(both, order)
            rows = [
                ordered[:, part * LANES : (part + 1) * LANES] * masks[part // 2]
                for part in range(4)
            ]
            columns.append(jnp.concatenate(rows, 0).astype(jnp.bfloat16))
    return kspace_back(jnp.concatenate(columns, 1), xi)


def kspace_step(portion, sampling, xf, xi):
    spectrum = product(xf, portion)
    columns = []
    for comp in range(sampling.shape[0]):
        masks = masks_of(sampling[comp])
        for pair in range(PAIRS):
            at = (comp * PAIRS + pair) * LANES
            rows = [
                spectrum[part * NX : (part + 1) * NX, at : at + LANES] * masks[part // 2]
                for part in range(4)
            ]
            columns.append(jnp.concatenate(rows, 0).astype(jnp.bfloat16))
    return kspace_back(jnp.concatenate(columns, 1), xi)


def combine_coils(arrived, factors, yi, zi):
    rows = product(yi, arrived).astype(jnp.bfloat16)
    images = []
    for comp in range(arrived.shape[1] // (PAIRS * LANES)):
        total = None
        for pair in range(PAIRS):
            at = (comp * PAIRS + pair) * LANES
            both = jnp.concatenate(
                [rows[: 2 * NY, at : at + LANES], rows[2 * NY :, at : at + LANES]], 1
            )
            depth = product(both, zi)
            for coil in range(2):
                real_map, turn_map = factors[2 * pair + coil]
                image = depth[:, coil * LANES : (coil + 1) * LANES]
                term = real_map * image - turn_map * swap_halves(image)
                total = term if total is None else total + term
        images.append(total)
    return images


def spread_out(images, factors, zf, yf):
    columns = []
    for image in images:
        turned = swap_halves(image)
        for pair in range(PAIRS):
            both = jnp.concatenate(
                [
                    (real_map * image + turn_map * turned).astype(jnp.bfloat16)
                    for real_map, turn_map in factors[2 * pair : 2 * pair + 2]
                ],
                1,
            )
            depth = product(both, zf).astype(jnp.bfloat16)
            columns.append(jnp.concatenate([depth[:, :LANES], depth[:, LANES:]], 0))
    return product(yf, jnp.concatenate(columns, 1)).astype(jnp.bfloat16)


def partial_dot(left, right):
    total = None
    for one, other in zip(left, right):
        folded = (one * other).reshape(-1, 8, LANES).sum(0)
        total = folded if total is None else total + folded
    return total


def first_kernel(kspace, sampling, order, xi, out):
    out[...] = first_step(kspace[...], sampling[...], order[...], xi[...])


def kspace_kernel(portion, sampling, xf, xi, out):
    out[...] = kspace_step(portion[...], sampling[...], xf[...], xi[...])


def image_kernel(*refs, earlier, onward):
    refs = list(refs)
    arrived, coils, yi, zi = refs[:4]
    refs = refs[4:]
    old = [refs.pop(0) for _ in range(earlier)]
    if onward:
        zf, yf = refs.pop(0), refs.pop(0)
    image_out, dots_out = refs[:2]
    factors = [coil_factors(coils[coil]) for coil in range(COILS)]
    images = combine_coils(arrived[...], factors, yi[...], zi[...])
    if onward:
        refs[2][...] = spread_out(images, factors, zf[...], yf[...])
    for comp, image in enumerate(images):
        image_out[comp] = image
    for place in range(earlier):
        dots_out[place] = partial_dot([old[place][comp] for comp in range(len(images))], images)
    if onward:
        dots_out[earlier] = partial_dot(images, images)


def call(body, operands, shapes, flops):
    held = sum(math.prod(o.shape) * o.dtype.itemsize for o in operands)
    held += sum(math.prod(s.shape) * s.dtype.itemsize for s in shapes)
    return pl.pallas_call(
        body,
        out_shape=shapes,
        in_specs=[pl.BlockSpec(memory_space=pltpu.VMEM)] * len(operands),
        out_specs=[pl.BlockSpec(memory_space=pltpu.VMEM)] * len(shapes),
        compiler_params=pltpu.CompilerParams(vmem_limit_bytes=32 * 1024 * 1024),
        cost_estimate=pl.CostEstimate(flops=flops, bytes_accessed=held, transcendentals=0),
    )(*operands)


def exchange(values):
    return lax.all_to_all(values, "slab", split_axis=0, concat_axis=0, tiled=True)


def total_of(values):
    devices = lax.axis_size("slab") * lax.axis_size("comp")
    row = jnp.zeros((1, 1, LANES), jnp.float32).at[0, 0, : values.shape[0]].set(values)
    handed = jnp.broadcast_to(row, (devices, 1, LANES))
    gathered = lax.all_to_all(handed, ("slab", "comp"), split_axis=0, concat_axis=0, tiled=True)
    return gathered.sum((0, 1))[: values.shape[0]]


def shards(kspace, sensitivities, sampling):
    comps_here = kspace.shape[0]
    tables = make_tables()
    tables = {name: jnp.asarray(value) for name, value in tables.items()}
    coils = sensitivities.reshape(COILS, 2, NY, LANES).transpose(0, 2, 1, 3)
    coils = coils.reshape(COILS, 2 * NY, LANES)
    starts = range(0, comps_here, CHUNK)
    patterns = [sampling[start : start + CHUNK] for start in starts]
    width = CHUNK * PAIRS * LANES
    sent_shape = jax.ShapeDtypeStruct((4 * NX, width), jnp.bfloat16)
    image_shape = jax.ShapeDtypeStruct((CHUNK, 2 * NY, LANES), jnp.float32)
    square = 2 * (4 * NX) * (4 * NX) * width

    def image_step(arrived, old, onward):
        operands = [arrived, coils, tables["yi"], tables["zi"], *old]
        shapes = [image_shape]
        shapes.append(jax.ShapeDtypeStruct((len(old) + onward, 8, LANES), jnp.float32))
        if onward:
            operands += [tables["zf"], tables["yf"]]
            shapes.append(sent_shape)
        body = functools.partial(image_kernel, earlier=len(old), onward=onward)
        return call(body, operands, shapes, 3 * square)

    sent = [
        call(
            first_kernel,
            [kspace[start : start + CHUNK], pattern, tables["order"], tables["xi"]],
            [sent_shape],
            2 * square,
        )[0]
        for start, pattern in zip(starts, patterns)
    ]
    chains = [[] for _ in starts]
    dots = [[] for _ in starts]
    for stage in range(3):
        if stage > 0:
            arrived = [exchange(values) for values in sent]
            sent = [
                call(kspace_kernel, [values, pattern, tables["xf"], tables["xi"]], [sent_shape], 2 * square)[0]
                for values, pattern in zip(arrived, patterns)
            ]
        arrived = [exchange(values) for values in sent]
        sent = []
        for place, values in enumerate(arrived):
            image, dot, *more = image_step(values, chains[place], stage < 2)
            chains[place].append(image)
            dots[place].append(dot)
            sent += more
    here = sum(jnp.concatenate(dot, 0) for dot in dots).sum((1, 2))
    bb, bq, qq, bt, qt = total_of(here)
    step_one = bb / bq
    norm_next = bb - 2.0 * step_one * bq + step_one * step_one * qq
    ratio = norm_next / bb
    more = 1.0 + ratio
    curve = more * more * bq - more * step_one * (bt + qq) + step_one * step_one * qt
    step_two = norm_next / curve
    images = [jnp.concatenate([chain[power] for chain in chains], 0) for power in range(3)]
    images = [
        image.reshape(comps_here, NY, 2, LANES).transpose(0, 2, 1, 3).reshape(comps_here, 2, -1)
        for image in images
    ]
    b, q, t = images
    along_b, along_q = step_one + step_two * more, step_two * step_one
    coefficients = along_b * b - along_q * q
    residual = b - along_b * q + along_q * t
    return (coefficients, residual)


def solution(mesh):
    in_specs = (P("comp", None, None, "slab"), P(None, "slab", None), P("comp", None, "slab"))
    out_specs = (P("comp", "slab", None), P("comp", "slab", None))
    return jax.shard_map(shards, mesh=mesh, in_specs=in_specs, out_specs=out_specs, check_vma=False)
```

```python
import math

import jax
import jax.numpy as jnp
import numpy as np
from jax import lax
from jax.experimental import pallas as pl
from jax.experimental.pallas import tpu as pltpu
from jax.sharding import PartitionSpec as P

NX = 128
NY = 128
NZ = 64
COILS = 4
PAIRS = COILS // 2
LANES = 2 * NZ


def fourier_blocks(length, orientation):
    positions = np.arange(length)
    angles = (positions[:, None] * positions[None, :] % length) * (2.0 * math.pi / length)
    scaling = 1.0 / math.sqrt(length)
    real_part = np.cos(angles) * scaling
    imaginary = orientation * np.sin(angles) * scaling
    top_rows = np.stack([real_part, -imaginary], 1)
    low_rows = np.stack([imaginary, real_part], 1)
    return np.stack([top_rows, low_rows], 0).astype(np.float32)


def table(spec, *factors, shape):
    return np.einsum(spec, *factors).reshape(shape).astype(jnp.bfloat16)


def make_tables():
    two = np.eye(2, dtype=np.float32)
    slabs = NX // 2
    zf, zi = fourier_blocks(NZ, -1.0), fourier_blocks(NZ, 1.0)
    yf, yi = fourier_blocks(NY, -1.0), fourier_blocks(NY, 1.0)
    xf = fourier_blocks(NX, -1.0).reshape(2, NX, 2, slabs, 2)
    xi = fourier_blocks(NX, 1.0).reshape(2, slabs, 2, 2, NX)
    return {
        "zf": table("akbj,cd->cbjadk", zf, two, shape=(4 * NZ, 4 * NZ)),
        "zi": table("akbj,cd->bcjdak", zi, two, shape=(4 * NZ, 4 * NZ)),
        "yf": table("akbj,cd->kcabjd", yf, two, shape=(4 * NY, 4 * NY)),
        "yi": table("akbj,cd->akcjdb", yi, two, shape=(4 * NY, 4 * NY)),
        "xf": table("akbst,cd->caksdtb", xf, two, shape=(4 * NX, 4 * NX)),
        "xi": table("astbk,cd->sctadbk", xi, two, shape=(4 * NX, 4 * NX)),
        "order": table(
            "ab,ef,gh->aegfbh", two, two, np.eye(NZ, dtype=np.float32), shape=(4 * NZ, 4 * NZ)
        ),
    }


def product(left, right):
    return jnp.dot(left, right, preferred_element_type=jnp.float32)


def swap_halves(values):
    return pltpu.roll(values, NZ, values.ndim - 1)


def low_half(shape):
    return lax.broadcasted_iota(jnp.int32, shape, len(shape) - 1) < NZ


def masks_of(sampling):
    pattern = sampling.astype(jnp.float32)
    other = swap_halves(pattern)
    low = low_half(pattern.shape)
    return jnp.where(low, pattern, other), jnp.where(low, other, pattern)


def coil_factors(maps):
    other = swap_halves(maps)
    low = low_half(maps.shape)
    return jnp.where(low, maps, other), jnp.where(low, -other, maps)


def first_masked(kspace, sampling, order):
    masks = masks_of(sampling)
    columns = []
    for pair in range(PAIRS):
        rows = []
        for place in range(2):
            lanes = slice(place * LANES, (place + 1) * LANES)
            both = jnp.concatenate([kspace[2 * pair][:, lanes], kspace[2 * pair + 1][:, lanes]], 1)
            ordered = product(both, order)
            rows += [ordered[:, :LANES] * masks[place], ordered[:, LANES:] * masks[place]]
        columns.append(jnp.concatenate(rows, 0).astype(jnp.bfloat16))
    return jnp.concatenate(columns, 1)


def masked_spectrum(portion, sampling, xf):
    spectrum = product(xf, portion)
    columns = []
    for comp in range(sampling.shape[0]):
        masks = masks_of(sampling[comp])
        for pair in range(PAIRS):
            at = (comp * PAIRS + pair) * LANES
            rows = [
                spectrum[part * NX : (part + 1) * NX, at : at + LANES] * masks[part // 2]
                for part in range(4)
            ]
            columns.append(jnp.concatenate(rows, 0).astype(jnp.bfloat16))
    return jnp.concatenate(columns, 1)


def combine_coils(arrived, factors, yi, zi):
    rows = product(yi, arrived).astype(jnp.bfloat16)
    images = []
    for comp in range(arrived.shape[1] // (PAIRS * LANES)):
        total = None
        for pair in range(PAIRS):
            at = (comp * PAIRS + pair) * LANES
            both = jnp.concatenate(
                [rows[: 2 * NY, at : at + LANES], rows[2 * NY :, at : at + LANES]], 1
            )
            depth = product(both, zi)
            for coil in range(2):
                real_map, turn_map = factors[2 * pair + coil]
                image = depth[:, coil * LANES : (coil + 1) * LANES]
                term = real_map * image - turn_map * swap_halves(image)
                total = term if total is None else total + term
        images.append(total)
    return images


def spread_out(images, factors, zf, yf):
    columns = []
    for image in images:
        turned = swap_halves(image)
        for pair in range(PAIRS):
            both = jnp.concatenate(
                [
                    (real_map * image + turn_map * turned).astype(jnp.bfloat16)
                    for real_map, turn_map in factors[2 * pair : 2 * pair + 2]
                ],
                1,
            )
            depth = product(both, zf).astype(jnp.bfloat16)
            columns.append(jnp.concatenate([depth[:, :LANES], depth[:, LANES:]], 0))
    return product(yf, jnp.concatenate(columns, 1)).astype(jnp.bfloat16)


def fold_rows(values):
    rows = values.sum(0, keepdims=True)
    return sum(rows[:, at : at + LANES] for at in range(0, rows.shape[1], LANES))


def row_of(one, other):
    return fold_rows(one.astype(jnp.float32) * other.astype(jnp.float32))


def final_scales(sums):
    totals = sums.sum(1, keepdims=True)
    bb, bq, qq, bt, qt = (totals[place : place + 1] for place in range(5))
    step_one = bb / bq
    norm_next = bb - 2.0 * step_one * bq + step_one * step_one * qq
    more = 1.0 + norm_next / bb
    curve = more * more * bq - more * step_one * (bt + qq) + step_one * step_one * qt
    step_two = norm_next / curve
    return step_one + step_two * more, step_two * step_one


def first_kernel(kspace_at, sampling_at, order_at, xi_at, out, kspace, sampling, order, xi, sems):
    copies = [pltpu.make_async_copy(order_at, order, sems.at[0])]
    copies.append(pltpu.make_async_copy(sampling_at, sampling, sems.at[1]))
    for comp in range(kspace.shape[0]):
        copies.append(pltpu.make_async_copy(kspace_at.at[comp], kspace.at[comp], sems.at[2 + comp]))
    copies.append(pltpu.make_async_copy(xi_at, xi, sems.at[2 + kspace.shape[0]]))
    for copy in copies:
        copy.start()
    copies[0].wait()
    copies[1].wait()
    columns = []
    for comp in range(kspace.shape[0]):
        copies[2 + comp].wait()
        columns.append(first_masked(kspace[comp], sampling[comp], order[...]))
    copies[-1].wait()
    out[...] = product(xi[...], jnp.concatenate(columns, 1)).astype(jnp.bfloat16)


def kspace_kernel(portion, sampling, xf, xi, out, masked_out, sum_out):
    masked = masked_spectrum(portion[...], sampling[...], xf[...])
    masked_out[...] = masked
    sum_out[...] = row_of(masked, masked)
    out[...] = product(xi[...], masked).astype(jnp.bfloat16)


def kspace_last_kernel(portion, sampling, xf, xi, masked_b, bb, bq, qq, out, sums_out):
    masked = masked_spectrum(portion[...], sampling[...], xf[...])
    out[...] = product(xi[...], masked).astype(jnp.bfloat16)
    sums_out[0:1] = bb[...]
    sums_out[1:2] = bq[...]
    sums_out[2:3] = qq[...]
    sums_out[3:4] = row_of(masked_b[...], masked)
    sums_out[4:5] = row_of(masked, masked)
    sums_out[5:8] = jnp.zeros((3, LANES), jnp.float32)


def image_kernel(arrived, coils, yi, zi, zf, yf, image_out, sum_out, out):
    factors = [coil_factors(coils[coil]) for coil in range(COILS)]
    images = combine_coils(arrived[...], factors, yi[...], zi[...])
    out[...] = spread_out(images, factors, zf[...], yf[...])
    for comp, image in enumerate(images):
        image_out[comp] = image
    sum_out[...] = sum(row_of(image, image) for image in images)


def last_kernel(arrived, coils, yi, zi, b, q, sums, coefficients, residual):
    factors = [coil_factors(coils[coil]) for coil in range(COILS)]
    images = combine_coils(arrived[...], factors, yi[...], zi[...])
    along_b, along_q = final_scales(sums[...])
    for comp, image in enumerate(images):
        coefficients[comp] = along_b * b[comp] - along_q * q[comp]
        residual[comp] = b[comp] - along_b * q[comp] + along_q * image


def call(body, operands, shapes, flops, space=pltpu.VMEM, scratch=()):
    held = sum(math.prod(o.shape) * o.dtype.itemsize for o in operands)
    held += sum(math.prod(s.shape) * s.dtype.itemsize for s in shapes)
    return pl.pallas_call(
        body,
        out_shape=shapes,
        in_specs=[pl.BlockSpec(memory_space=space)] * len(operands),
        out_specs=[pl.BlockSpec(memory_space=pltpu.VMEM)] * len(shapes),
        scratch_shapes=scratch,
        compiler_params=pltpu.CompilerParams(vmem_limit_bytes=32 * 1024 * 1024),
        cost_estimate=pl.CostEstimate(flops=flops, bytes_accessed=held, transcendentals=0),
    )(*operands)


def exchange(values):
    return lax.all_to_all(values, "slab", split_axis=0, concat_axis=0, tiled=True)


def exclusive(axis, flips):
    return [(place, place ^ flips) for place in range(lax.axis_size(axis))]


def total_of(values):
    for axis, low in (("comp", 1), ("slab", 1), ("slab", 4), ("slab", 16)):
        one, two, three = (
            lax.ppermute(values, axis, exclusive(axis, flips * low)) for flips in (1, 2, 3)
        )
        values = (values + one) + (two + three)
    return values


def shards(kspace, sensitivities, sampling):
    comps = kspace.shape[0]
    tables = {name: jnp.asarray(value) for name, value in make_tables().items()}
    coils = sensitivities.reshape(COILS, 2, NY, LANES).transpose(0, 2, 1, 3)
    coils = coils.reshape(COILS, 2 * NY, LANES)
    width = comps * PAIRS * LANES
    sent_shape = jax.ShapeDtypeStruct((4 * NX, width), jnp.bfloat16)
    image_shape = jax.ShapeDtypeStruct((comps, 2 * NY, LANES), jnp.float32)
    sum_shape = jax.ShapeDtypeStruct((1, LANES), jnp.float32)
    sums_shape = jax.ShapeDtypeStruct((8, LANES), jnp.float32)
    square = 2 * (4 * NX) * (4 * NX) * width

    def image_step(arrived):
        operands = [arrived, coils] + [tables[name] for name in ("yi", "zi", "zf", "yf")]
        return call(image_kernel, operands, [image_shape, sum_shape, sent_shape], 3 * square)

    first = [kspace, sampling, tables["order"], tables["xi"]]
    scratch = [pltpu.VMEM(array.shape, array.dtype) for array in first]
    scratch.append(pltpu.SemaphoreType.DMA((3 + comps,)))
    (sent,) = call(first_kernel, first, [sent_shape], 2 * square, pltpu.HBM, scratch)
    b, bb, sent = image_step(exchange(sent))
    operands = [exchange(sent), sampling, tables["xf"], tables["xi"]]
    sent, masked_b, bq = call(
        kspace_kernel, operands, [sent_shape, sent_shape, sum_shape], 2 * square
    )
    q, qq, sent = image_step(exchange(sent))
    operands = [exchange(sent), sampling, tables["xf"], tables["xi"], masked_b, bb, bq, qq]
    sent, sums = call(kspace_last_kernel, operands, [sent_shape, sums_shape], 2 * square)
    arrived = exchange(sent)
    operands = [arrived, coils, tables["yi"], tables["zi"], b, q, total_of(sums)]
    outputs = call(last_kernel, operands, [image_shape] * 2, 2 * square)
    return tuple(
        output.reshape(comps, NY, 2, LANES).transpose(0, 2, 1, 3).reshape(comps, 2, -1)
        for output in outputs
    )


def solution(mesh):
    in_specs = (P("comp", None, None, "slab"), P(None, "slab", None), P("comp", None, "slab"))
    out_specs = (P("comp", "slab", None), P("comp", "slab", None))
    return jax.shard_map(shards, mesh=mesh, in_specs=in_specs, out_specs=out_specs, check_vma=False)
```

```python
import math

import jax
import jax.numpy as jnp
import numpy as np
from jax import lax
from jax.experimental import pallas as pl
from jax.experimental.pallas import tpu as pltpu
from jax.sharding import PartitionSpec as P

NX = 128
NY = 128
NZ = 64
COILS = 4
PAIRS = COILS // 2
LANES = 2 * NZ
STEPS = (("comp", 1, 4), ("slab", 1, 4), ("slab", 4, 4), ("slab", 16, 4))


def fourier_blocks(length, orientation):
    positions = np.arange(length)
    angles = (positions[:, None] * positions[None, :] % length) * (2.0 * math.pi / length)
    scaling = 1.0 / math.sqrt(length)
    real_part = np.cos(angles) * scaling
    imaginary = orientation * np.sin(angles) * scaling
    top_rows = np.stack([real_part, -imaginary], 1)
    low_rows = np.stack([imaginary, real_part], 1)
    return np.stack([top_rows, low_rows], 0).astype(np.float32)


def table(spec, *factors, shape):
    return np.einsum(spec, *factors).reshape(shape).astype(jnp.bfloat16)


def make_tables():
    two = np.eye(2, dtype=np.float32)
    slabs = NX // 2
    zf, zi = fourier_blocks(NZ, -1.0), fourier_blocks(NZ, 1.0)
    yf, yi = fourier_blocks(NY, -1.0), fourier_blocks(NY, 1.0)
    xf = fourier_blocks(NX, -1.0).reshape(2, NX, 2, slabs, 2)
    xi = fourier_blocks(NX, 1.0).reshape(2, slabs, 2, 2, NX)
    return {
        "zf": table("akbj,cd->cbjadk", zf, two, shape=(4 * NZ, 4 * NZ)),
        "zi": table("akbj,cd->bcjdak", zi, two, shape=(4 * NZ, 4 * NZ)),
        "yf": table("akbj,cd->kcabjd", yf, two, shape=(4 * NY, 4 * NY)),
        "yi": table("akbj,cd->akcjdb", yi, two, shape=(4 * NY, 4 * NY)),
        "xf": table("akbst,cd->caksdtb", xf, two, shape=(4 * NX, 4 * NX)),
        "xi": table("astbk,cd->sctadbk", xi, two, shape=(4 * NX, 4 * NX)),
        "order": table(
            "ab,ef,gh->aegfbh", two, two, np.eye(NZ, dtype=np.float32), shape=(4 * NZ, 4 * NZ)
        ),
    }


def product(left, right):
    return jnp.dot(left, right, preferred_element_type=jnp.float32)


def swap_halves(values):
    return pltpu.roll(values, NZ, values.ndim - 1)


def low_half(shape):
    return lax.broadcasted_iota(jnp.int32, shape, len(shape) - 1) < NZ


def masks_of(sampling):
    pattern = sampling.astype(jnp.float32)
    other = swap_halves(pattern)
    low = low_half(pattern.shape)
    return jnp.where(low, pattern, other), jnp.where(low, other, pattern)


def coil_factors(maps):
    other = swap_halves(maps)
    low = low_half(maps.shape)
    return jnp.where(low, maps, other), jnp.where(low, -other, maps)


def first_masked(kspace, sampling, order):
    masks = masks_of(sampling)
    stacked = [
        jnp.concatenate(
            [kspace[coil][:, place * LANES : (place + 1) * LANES] for coil in (2 * pair, 2 * pair + 1)], 1
        )
        for pair in range(PAIRS)
        for place in range(2)
    ]
    ordered = product(jnp.concatenate(stacked, 0), order)
    columns = []
    for pair in range(PAIRS):
        rows = []
        for place in range(2):
            at = (2 * pair + place) * NX
            rows += [
                ordered[at : at + NX, part * LANES : (part + 1) * LANES] * masks[place]
                for part in range(2)
            ]
        columns.append(jnp.concatenate(rows, 0).astype(jnp.bfloat16))
    return jnp.concatenate(columns, 1)


def masked_spectrum(portion, sampling, xf):
    spectrum = product(xf, portion)
    columns = []
    for comp in range(sampling.shape[0]):
        masks = masks_of(sampling[comp])
        for pair in range(PAIRS):
            at = (comp * PAIRS + pair) * LANES
            rows = [
                spectrum[part * NX : (part + 1) * NX, at : at + LANES] * masks[part // 2]
                for part in range(4)
            ]
            columns.append(jnp.concatenate(rows, 0).astype(jnp.bfloat16))
    return jnp.concatenate(columns, 1)


def combine_coils(arrived, factors, yi, zi):
    rows = product(yi, arrived).astype(jnp.bfloat16)
    half = 2 * NY
    places = range(0, arrived.shape[1], LANES)
    stacked = [
        jnp.concatenate([rows[:half, at : at + LANES], rows[half:, at : at + LANES]], 1)
        for at in places
    ]
    depth = product(jnp.concatenate(stacked, 0), zi)
    images = []
    for comp in range(len(places) // PAIRS):
        total = None
        for coil in range(COILS):
            at = (comp * PAIRS + coil // 2) * half
            image = depth[at : at + half, coil % 2 * LANES : (coil % 2 + 1) * LANES]
            real_map, turn_map = factors[coil]
            term = real_map * image - turn_map * swap_halves(image)
            total = term if total is None else total + term
        images.append(total)
    return images


def spread_out(images, factors, zf, yf):
    half = 2 * NY
    stacked = []
    for image in images:
        turned = swap_halves(image)
        spread = [
            (real_map * image + turn_map * turned).astype(jnp.bfloat16)
            for real_map, turn_map in factors
        ]
        stacked += [jnp.concatenate(spread[2 * pair : 2 * pair + 2], 1) for pair in range(PAIRS)]
    depth = product(jnp.concatenate(stacked, 0), zf).astype(jnp.bfloat16)
    columns = [
        jnp.concatenate([depth[at : at + half, :LANES], depth[at : at + half, LANES:]], 0)
        for at in range(0, depth.shape[0], half)
    ]
    return product(yf, jnp.concatenate(columns, 1)).astype(jnp.bfloat16)


def fold_rows(values):
    rows = values.sum(0, keepdims=True)
    return sum(rows[:, at : at + LANES] for at in range(0, rows.shape[1], LANES))


def row_of(one, other):
    return fold_rows(one.astype(jnp.float32) * other.astype(jnp.float32))


def final_scales(sums):
    totals = sums.sum(1, keepdims=True)
    bb, bq, qq, bt, qt = (totals[place : place + 1] for place in range(5))
    step_one = bb / bq
    norm_next = bb - 2.0 * step_one * bq + step_one * step_one * qq
    more = 1.0 + norm_next / bb
    curve = more * more * bq - more * step_one * (bt + qq) + step_one * step_one * qt
    step_two = norm_next / curve
    return step_one + step_two * more, step_two * step_one


def first_kernel(kspace_at, sampling_at, order_at, xi_at, out, kspace, sampling, order, xi, sems):
    copies = [pltpu.make_async_copy(order_at, order, sems.at[0])]
    copies.append(pltpu.make_async_copy(sampling_at, sampling, sems.at[1]))
    for comp in range(kspace.shape[0]):
        copies.append(pltpu.make_async_copy(kspace_at.at[comp], kspace.at[comp], sems.at[2 + comp]))
    copies.append(pltpu.make_async_copy(xi_at, xi, sems.at[2 + kspace.shape[0]]))
    for copy in copies:
        copy.start()
    copies[0].wait()
    copies[1].wait()
    columns = []
    for comp in range(kspace.shape[0]):
        copies[2 + comp].wait()
        columns.append(first_masked(kspace[comp], sampling[comp], order[...]))
    copies[-1].wait()
    out[...] = product(xi[...], jnp.concatenate(columns, 1)).astype(jnp.bfloat16)


def kspace_kernel(portion, sampling, xf, xi, out, masked_out, sum_out):
    masked = masked_spectrum(portion[...], sampling[...], xf[...])
    masked_out[...] = masked
    sum_out[...] = row_of(masked, masked)
    out[...] = product(xi[...], masked).astype(jnp.bfloat16)


def kspace_last_kernel(portion, sampling, xf, xi, masked_b, bb, bq, qq, out, sums_out):
    masked = masked_spectrum(portion[...], sampling[...], xf[...])
    out[...] = product(xi[...], masked).astype(jnp.bfloat16)
    sums_out[0:1] = bb[...]
    sums_out[1:2] = bq[...]
    sums_out[2:3] = qq[...]
    sums_out[3:4] = row_of(masked_b[...], masked)
    sums_out[4:5] = row_of(masked, masked)
    sums_out[5:8] = jnp.zeros((3, LANES), jnp.float32)


def image_kernel(arrived, coils, yi, zi, zf, yf, image_out, sum_out, out):
    factors = [coil_factors(coils[coil]) for coil in range(COILS)]
    images = combine_coils(arrived[...], factors, yi[...], zi[...])
    out[...] = spread_out(images, factors, zf[...], yf[...])
    for comp, image in enumerate(images):
        image_out[comp] = image
    sum_out[...] = sum(row_of(image, image) for image in images)


def last_kernel(arrived, coils, yi, zi, b, q, sums, coefficients, residual):
    factors = [coil_factors(coils[coil]) for coil in range(COILS)]
    images = combine_coils(arrived[...], factors, yi[...], zi[...])
    along_b, along_q = final_scales(sums[...])
    for comp, image in enumerate(images):
        coefficients[comp] = along_b * b[comp] - along_q * q[comp]
        residual[comp] = b[comp] - along_b * q[comp] + along_q * image


def call(body, operands, shapes, flops, space=pltpu.VMEM, scratch=(), mebibytes=32):
    held = sum(math.prod(o.shape) * o.dtype.itemsize for o in operands)
    held += sum(math.prod(s.shape) * s.dtype.itemsize for s in shapes)
    return pl.pallas_call(
        body,
        out_shape=shapes,
        in_specs=[pl.BlockSpec(memory_space=space)] * len(operands),
        out_specs=[pl.BlockSpec(memory_space=pltpu.VMEM)] * len(shapes),
        scratch_shapes=scratch,
        compiler_params=pltpu.CompilerParams(vmem_limit_bytes=mebibytes * 1024 * 1024),
        cost_estimate=pl.CostEstimate(flops=flops, bytes_accessed=held, transcendentals=0),
    )(*operands)


def exchange(values):
    return lax.all_to_all(values, "slab", split_axis=0, concat_axis=0, tiled=True)


def exclusive(axis, flips):
    return [(place, place ^ flips) for place in range(lax.axis_size(axis))]


def sum_over(values, axis, low, count):
    terms = [values]
    terms += [lax.ppermute(values, axis, exclusive(axis, flips * low)) for flips in range(1, count)]
    while len(terms) > 1:
        terms = [one + other for one, other in zip(terms[::2], terms[1::2])]
    return terms[0]


def total_of(values):
    for axis, low, count in STEPS:
        values = sum_over(values, axis, low, count)
    return values


def shards(kspace, sensitivities, sampling):
    comps = kspace.shape[0]
    tables = {name: jnp.asarray(value) for name, value in make_tables().items()}
    coils = sensitivities.reshape(COILS, 2, NY, LANES).transpose(0, 2, 1, 3)
    coils = coils.reshape(COILS, 2 * NY, LANES)
    width = comps * PAIRS * LANES
    sent_shape = jax.ShapeDtypeStruct((4 * NX, width), jnp.bfloat16)
    image_shape = jax.ShapeDtypeStruct((comps, 2 * NY, LANES), jnp.float32)
    sum_shape = jax.ShapeDtypeStruct((1, LANES), jnp.float32)
    sums_shape = jax.ShapeDtypeStruct((8, LANES), jnp.float32)
    square = 2 * (4 * NX) * (4 * NX) * width

    def image_step(arrived):
        operands = [arrived, coils] + [tables[name] for name in ("yi", "zi", "zf", "yf")]
        return call(image_kernel, operands, [image_shape, sum_shape, sent_shape], 3 * square)

    first = [kspace, sampling, tables["order"], tables["xi"]]
    scratch = [pltpu.VMEM(array.shape, array.dtype) for array in first]
    scratch.append(pltpu.SemaphoreType.DMA((3 + comps,)))
    (sent,) = call(first_kernel, first, [sent_shape], 2 * square, pltpu.HBM, scratch, 58)
    b, bb, sent = image_step(exchange(sent))
    operands = [exchange(sent), sampling, tables["xf"], tables["xi"]]
    sent, masked_b, bq = call(
        kspace_kernel, operands, [sent_shape, sent_shape, sum_shape], 2 * square
    )
    q, qq, sent = image_step(exchange(sent))
    operands = [exchange(sent), sampling, tables["xf"], tables["xi"], masked_b, bb, bq, qq]
    sent, sums = call(kspace_last_kernel, operands, [sent_shape, sums_shape], 2 * square)
    arrived = exchange(sent)
    operands = [arrived, coils, tables["yi"], tables["zi"], b, q, total_of(sums)]
    outputs = call(last_kernel, operands, [image_shape] * 2, 2 * square)
    return tuple(
        output.reshape(comps, NY, 2, LANES).transpose(0, 2, 1, 3).reshape(comps, 2, -1)
        for output in outputs
    )


def solution(mesh):
    in_specs = (P("comp", None, None, "slab"), P(None, "slab", None), P("comp", None, "slab"))
    out_specs = (P("comp", "slab", None), P("comp", "slab", None))
    return jax.shard_map(shards, mesh=mesh, in_specs=in_specs, out_specs=out_specs, check_vma=False)
```

```python
import math

import jax
import jax.numpy as jnp
import numpy as np
from jax import lax
from jax.experimental import pallas as pl
from jax.experimental.pallas import tpu as pltpu
from jax.sharding import PartitionSpec as P

NX = 128
NY = 128
NZ = 64
COILS = 4
PAIRS = COILS // 2
LANES = 2 * NZ
GROUP_STEPS = (("slab", 1, 4), ("slab", 4, 4), ("slab", 16, 4))
STEPS = (("comp", 1, 4),) + GROUP_STEPS


def fourier_blocks(length, orientation):
    positions = np.arange(length)
    angles = (positions[:, None] * positions[None, :] % length) * (2.0 * math.pi / length)
    scaling = 1.0 / math.sqrt(length)
    real_part = np.cos(angles) * scaling
    imaginary = orientation * np.sin(angles) * scaling
    top_rows = np.stack([real_part, -imaginary], 1)
    low_rows = np.stack([imaginary, real_part], 1)
    return np.stack([top_rows, low_rows], 0).astype(np.float32)


def table(spec, *factors, shape):
    return np.einsum(spec, *factors).reshape(shape).astype(jnp.bfloat16)


def make_tables():
    two = np.eye(2, dtype=np.float32)
    slabs = NX // 2
    zf, zi = fourier_blocks(NZ, -1.0), fourier_blocks(NZ, 1.0)
    yf, yi = fourier_blocks(NY, -1.0), fourier_blocks(NY, 1.0)
    xf = fourier_blocks(NX, -1.0).reshape(2, NX, 2, slabs, 2)
    xi = fourier_blocks(NX, 1.0).reshape(2, slabs, 2, 2, NX)
    return {
        "zf": table("akbj,cd->cbjadk", zf, two, shape=(4 * NZ, 4 * NZ)),
        "zi": table("akbj,cd->bcjdak", zi, two, shape=(4 * NZ, 4 * NZ)),
        "yf": table("akbj,cd->kcabjd", yf, two, shape=(4 * NY, 4 * NY)),
        "yi": table("akbj,cd->akcjdb", yi, two, shape=(4 * NY, 4 * NY)),
        "xf": table("akbst,cd->caksdtb", xf, two, shape=(4 * NX, 4 * NX)),
        "xi": table("astbk,cd->sctadbk", xi, two, shape=(4 * NX, 4 * NX)),
        "order": table(
            "ab,ef,gh->aegfbh", two, two, np.eye(NZ, dtype=np.float32), shape=(4 * NZ, 4 * NZ)
        ),
    }


def product(left, right):
    return jnp.dot(left, right, preferred_element_type=jnp.float32)


def swap_halves(values):
    return pltpu.roll(values, NZ, values.ndim - 1)


def low_half(shape):
    return lax.broadcasted_iota(jnp.int32, shape, len(shape) - 1) < NZ


def masks_of(sampling):
    pattern = sampling.astype(jnp.float32)
    other = swap_halves(pattern)
    low = low_half(pattern.shape)
    return jnp.where(low, pattern, other), jnp.where(low, other, pattern)


def coil_factors(maps):
    other = swap_halves(maps)
    low = low_half(maps.shape)
    return jnp.where(low, maps, other), jnp.where(low, -other, maps)


def first_masked(kspace, sampling, order):
    masks = masks_of(sampling)
    stacked = [
        jnp.concatenate(
            [kspace[coil][:, place * LANES : (place + 1) * LANES] for coil in (2 * pair, 2 * pair + 1)], 1
        )
        for pair in range(PAIRS)
        for place in range(2)
    ]
    ordered = product(jnp.concatenate(stacked, 0), order)
    columns = []
    for pair in range(PAIRS):
        rows = []
        for place in range(2):
            at = (2 * pair + place) * NX
            rows += [
                ordered[at : at + NX, part * LANES : (part + 1) * LANES] * masks[place]
                for part in range(2)
            ]
        columns.append(jnp.concatenate(rows, 0).astype(jnp.bfloat16))
    return jnp.concatenate(columns, 1)


def masked_spectrum(portion, sampling, xf):
    spectrum = product(xf, portion)
    columns = []
    for comp in range(sampling.shape[0]):
        masks = masks_of(sampling[comp])
        for pair in range(PAIRS):
            at = (comp * PAIRS + pair) * LANES
            rows = [
                spectrum[part * NX : (part + 1) * NX, at : at + LANES] * masks[part // 2]
                for part in range(4)
            ]
            columns.append(jnp.concatenate(rows, 0).astype(jnp.bfloat16))
    return jnp.concatenate(columns, 1)


def combine_coils(arrived, factors, yi, zi):
    rows = product(yi, arrived).astype(jnp.bfloat16)
    half = 2 * NY
    places = range(0, arrived.shape[1], LANES)
    stacked = [
        jnp.concatenate([rows[:half, at : at + LANES], rows[half:, at : at + LANES]], 1)
        for at in places
    ]
    depth = product(jnp.concatenate(stacked, 0), zi)
    images = []
    for comp in range(len(places) // PAIRS):
        straight = turned = None
        for coil in range(COILS):
            at = (comp * PAIRS + coil // 2) * half
            image = depth[at : at + half, coil % 2 * LANES : (coil % 2 + 1) * LANES]
            real_map, turn_map = factors[coil]
            straight = real_map * image if coil == 0 else straight + real_map * image
            turned = turn_map * image if coil == 0 else turned + turn_map * image
        images.append(straight + swap_halves(turned))
    return images


def spread_out(images, factors, zf, yf):
    half = 2 * NY
    stacked = []
    for image in images:
        turned = swap_halves(image)
        spread = [
            (real_map * image + turn_map * turned).astype(jnp.bfloat16)
            for real_map, turn_map in factors
        ]
        stacked += [jnp.concatenate(spread[2 * pair : 2 * pair + 2], 1) for pair in range(PAIRS)]
    depth = product(jnp.concatenate(stacked, 0), zf).astype(jnp.bfloat16)
    columns = [
        jnp.concatenate([depth[at : at + half, :LANES], depth[at : at + half, LANES:]], 0)
        for at in range(0, depth.shape[0], half)
    ]
    return product(yf, jnp.concatenate(columns, 1)).astype(jnp.bfloat16)


def fold_rows(values):
    rows = values.sum(0, keepdims=True)
    return sum(rows[:, at : at + LANES] for at in range(0, rows.shape[1], LANES))


def row_of(one, other):
    return fold_rows(one.astype(jnp.float32) * other.astype(jnp.float32))


def group_step(sums):
    totals = sums[0:2].sum(1, keepdims=True)
    bb, bq = totals[0:1], totals[1:2]
    usable = jnp.logical_and(bb > 0.0, bq > 0.0)
    return jnp.where(usable, bb, 1.0) / jnp.where(usable, bq, 1.0)


def final_scales(sums):
    totals = sums.sum(1, keepdims=True)
    bb, bq, qq, mixed, square = (totals[place : place + 1] for place in range(5))
    step_one = bb / bq
    norm_next = bb - 2.0 * step_one * bq + step_one * step_one * qq
    more = 1.0 + norm_next / bb
    curve = more * more * bq + 2.0 * more * step_one * mixed + step_one * step_one * square
    step_two = norm_next / curve
    return step_one + step_two * more, step_two * step_one


def first_kernel(kspace_at, sampling_at, order_at, xi_at, out, kspace, sampling, order, xi, sems):
    copies = [pltpu.make_async_copy(order_at, order, sems.at[0])]
    copies.append(pltpu.make_async_copy(sampling_at, sampling, sems.at[1]))
    for comp in range(kspace.shape[0]):
        copies.append(pltpu.make_async_copy(kspace_at.at[comp], kspace.at[comp], sems.at[2 + comp]))
    copies.append(pltpu.make_async_copy(xi_at, xi, sems.at[2 + kspace.shape[0]]))
    for copy in copies:
        copy.start()
    copies[0].wait()
    copies[1].wait()
    columns = []
    for comp in range(kspace.shape[0]):
        copies[2 + comp].wait()
        columns.append(first_masked(kspace[comp], sampling[comp], order[...]))
    copies[-1].wait()
    out[...] = product(xi[...], jnp.concatenate(columns, 1)).astype(jnp.bfloat16)


def kspace_kernel(portion, sampling, xf, xi, bb, out, masked_out, sums_out):
    masked = masked_spectrum(portion[...], sampling[...], xf[...])
    masked_out[...] = masked
    sums_out[0:1] = bb[...]
    sums_out[1:2] = row_of(masked, masked)
    sums_out[2:8] = jnp.zeros((6, LANES), jnp.float32)
    out[...] = product(xi[...], masked).astype(jnp.bfloat16)


def kspace_last_kernel(portion, sampling, xf, xi, masked_b, here, group, qq, out, sums_out):
    masked = masked_spectrum(portion[...], sampling[...], xf[...])
    out[...] = product(xi[...], masked).astype(jnp.bfloat16)
    inverse_step = 1.0 / group_step(group[...])
    earlier = masked_b[...].astype(jnp.float32)
    change = (masked.astype(jnp.float32) - earlier) * inverse_step
    sums_out[0:2] = here[0:2]
    sums_out[2:3] = qq[...]
    sums_out[3:4] = row_of(earlier, change)
    sums_out[4:5] = row_of(change, change)
    sums_out[5:8] = jnp.zeros((3, LANES), jnp.float32)


def image_kernel(arrived, coils, yi, zi, zf, yf, *refs):
    image_out, sum_out, out = refs[-3:]
    factors = [coil_factors(coils[coil]) for coil in range(COILS)]
    images = combine_coils(arrived[...], factors, yi[...], zi[...])
    for comp, image in enumerate(images):
        image_out[comp] = image
    sum_out[...] = sum(row_of(image, image) for image in images)
    if len(refs) > 3:
        b, group = refs[:2]
        step = group_step(group[...])
        images = [b[comp] - step * image for comp, image in enumerate(images)]
    out[...] = spread_out(images, factors, zf[...], yf[...])


def last_kernel(arrived, coils, yi, zi, b, q, group, sums, coefficients, residual):
    factors = [coil_factors(coils[coil]) for coil in range(COILS)]
    images = combine_coils(arrived[...], factors, yi[...], zi[...])
    along_b, along_q = final_scales(sums[...])
    along_t = along_q / group_step(group[...])
    for comp, image in enumerate(images):
        coefficients[comp] = along_b * b[comp] - along_q * q[comp]
        residual[comp] = b[comp] - along_b * q[comp] + along_t * (q[comp] - image)


def call(body, operands, shapes, flops, space=pltpu.VMEM, scratch=(), mebibytes=32):
    held = sum(math.prod(o.shape) * o.dtype.itemsize for o in operands)
    held += sum(math.prod(s.shape) * s.dtype.itemsize for s in shapes)
    return pl.pallas_call(
        body,
        out_shape=shapes,
        in_specs=[pl.BlockSpec(memory_space=space)] * len(operands),
        out_specs=[pl.BlockSpec(memory_space=pltpu.VMEM)] * len(shapes),
        scratch_shapes=scratch,
        compiler_params=pltpu.CompilerParams(vmem_limit_bytes=mebibytes * 1024 * 1024),
        cost_estimate=pl.CostEstimate(flops=flops, bytes_accessed=held, transcendentals=0),
    )(*operands)


def exchange(values):
    return lax.all_to_all(values, "slab", split_axis=0, concat_axis=0, tiled=True)


def exclusive(axis, flips):
    return [(place, place ^ flips) for place in range(lax.axis_size(axis))]


def sum_over(values, axis, low, count):
    terms = [values]
    terms += [lax.ppermute(values, axis, exclusive(axis, flips * low)) for flips in range(1, count)]
    while len(terms) > 1:
        terms = [one + other for one, other in zip(terms[::2], terms[1::2])]
    return terms[0]


def total_of(values, steps):
    for axis, low, count in steps:
        values = sum_over(values, axis, low, count)
    return values


def shards(kspace, sensitivities, sampling):
    comps = kspace.shape[0]
    tables = {name: jnp.asarray(value) for name, value in make_tables().items()}
    coils = sensitivities.reshape(COILS, 2, NY, LANES).transpose(0, 2, 1, 3)
    coils = coils.reshape(COILS, 2 * NY, LANES)
    width = comps * PAIRS * LANES
    sent_shape = jax.ShapeDtypeStruct((4 * NX, width), jnp.bfloat16)
    image_shape = jax.ShapeDtypeStruct((comps, 2 * NY, LANES), jnp.float32)
    sum_shape = jax.ShapeDtypeStruct((1, LANES), jnp.float32)
    sums_shape = jax.ShapeDtypeStruct((8, LANES), jnp.float32)
    square = 2 * (4 * NX) * (4 * NX) * width

    def image_step(arrived, *earlier):
        operands = [arrived, coils] + [tables[name] for name in ("yi", "zi", "zf", "yf")]
        operands += earlier
        return call(image_kernel, operands, [image_shape, sum_shape, sent_shape], 3 * square)

    first = [kspace, sampling, tables["order"], tables["xi"]]
    scratch = [pltpu.VMEM(array.shape, array.dtype) for array in first]
    scratch.append(pltpu.SemaphoreType.DMA((3 + comps,)))
    (sent,) = call(first_kernel, first, [sent_shape], 2 * square, pltpu.HBM, scratch, 58)
    b, bb, sent = image_step(exchange(sent))
    operands = [exchange(sent), sampling, tables["xf"], tables["xi"], bb]
    sent, masked_b, here = call(
        kspace_kernel, operands, [sent_shape, sent_shape, sums_shape], 2 * square
    )
    group = total_of(here, GROUP_STEPS)
    q, qq, sent = image_step(exchange(sent), b, group)
    operands = [exchange(sent), sampling, tables["xf"], tables["xi"], masked_b, here, group, qq]
    sent, sums = call(kspace_last_kernel, operands, [sent_shape, sums_shape], 2 * square)
    arrived = exchange(sent)
    operands = [arrived, coils, tables["yi"], tables["zi"], b, q, group, total_of(sums, STEPS)]
    outputs = call(last_kernel, operands, [image_shape] * 2, 2 * square)
    return tuple(
        output.reshape(comps, NY, 2, LANES).transpose(0, 2, 1, 3).reshape(comps, 2, -1)
        for output in outputs
    )


def solution(mesh):
    in_specs = (P("comp", None, None, "slab"), P(None, "slab", None), P("comp", None, "slab"))
    out_specs = (P("comp", "slab", None), P("comp", "slab", None))
    return jax.shard_map(shards, mesh=mesh, in_specs=in_specs, out_specs=out_specs, check_vma=False)
```

```python
import math

import jax
import jax.numpy as jnp
import numpy as np
from jax import lax
from jax.experimental import pallas as pl
from jax.experimental.pallas import tpu as pltpu
from jax.sharding import PartitionSpec as P

NX = 128
NY = 128
NZ = 64
COILS = 4
PAIRS = COILS // 2
LANES = 2 * NZ
GROUP_STEPS = (("slab", 1, 4), ("slab", 4, 4), ("slab", 16, 4))
STEPS = (("comp", 1, 4),) + GROUP_STEPS


def fourier_blocks(length, orientation):
    positions = np.arange(length)
    angles = (positions[:, None] * positions[None, :] % length) * (2.0 * math.pi / length)
    scaling = 1.0 / math.sqrt(length)
    real_part = np.cos(angles) * scaling
    imaginary = orientation * np.sin(angles) * scaling
    top_rows = np.stack([real_part, -imaginary], 1)
    low_rows = np.stack([imaginary, real_part], 1)
    return np.stack([top_rows, low_rows], 0).astype(np.float32)


def table(spec, *factors, shape):
    return np.einsum(spec, *factors).reshape(shape).astype(jnp.bfloat16)


def make_tables():
    two = np.eye(2, dtype=np.float32)
    slabs = NX // 2
    zf, zi = fourier_blocks(NZ, -1.0), fourier_blocks(NZ, 1.0)
    yf, yi = fourier_blocks(NY, -1.0), fourier_blocks(NY, 1.0)
    xf = fourier_blocks(NX, -1.0).reshape(2, NX, 2, slabs, 2)
    xi = fourier_blocks(NX, 1.0).reshape(2, slabs, 2, 2, NX)
    return {
        "zf": table("akbj,cd->cbjadk", zf, two, shape=(4 * NZ, 4 * NZ)),
        "zi": table("akbj,cd->bcjdak", zi, two, shape=(4 * NZ, 4 * NZ)),
        "yf": table("akbj,cd->kcabjd", yf, two, shape=(4 * NY, 4 * NY)),
        "yi": table("akbj,cd->akcjdb", yi, two, shape=(4 * NY, 4 * NY)),
        "xf": table("akbst,cd->caksdtb", xf, two, shape=(4 * NX, 4 * NX)),
        "xi": table("astbk,cd->sctadbk", xi, two, shape=(4 * NX, 4 * NX)),
        "order": table(
            "ab,ef,gh->aegfbh", two, two, np.eye(NZ, dtype=np.float32), shape=(4 * NZ, 4 * NZ)
        ),
    }


def product(left, right):
    return jnp.dot(left, right, preferred_element_type=jnp.float32)


def swap_halves(values):
    return pltpu.roll(values, NZ, values.ndim - 1)


def low_half(shape):
    return lax.broadcasted_iota(jnp.int32, shape, len(shape) - 1) < NZ


def masks_of(sampling):
    pattern = sampling.astype(jnp.float32)
    other = swap_halves(pattern)
    low = low_half(pattern.shape)
    return jnp.where(low, pattern, other), jnp.where(low, other, pattern)


def coil_factors(maps):
    other = swap_halves(maps)
    low = low_half(maps.shape)
    return jnp.where(low, maps, other), jnp.where(low, -other, maps)


def first_masked(kspace, sampling, order):
    masks = masks_of(sampling)
    stacked = [
        jnp.concatenate(
            [kspace[coil][:, place * LANES : (place + 1) * LANES] for coil in (2 * pair, 2 * pair + 1)], 1
        )
        for pair in range(PAIRS)
        for place in range(2)
    ]
    ordered = product(jnp.concatenate(stacked, 0), order)
    columns = []
    for pair in range(PAIRS):
        rows = []
        for place in range(2):
            at = (2 * pair + place) * NX
            rows += [
                ordered[at : at + NX, part * LANES : (part + 1) * LANES] * masks[place]
                for part in range(2)
            ]
        columns.append(jnp.concatenate(rows, 0).astype(jnp.bfloat16))
    return jnp.concatenate(columns, 1)


def masked_spectrum(portion, sampling, xf):
    spectrum = product(xf, portion)
    columns = []
    for comp in range(sampling.shape[0]):
        masks = masks_of(sampling[comp])
        for pair in range(PAIRS):
            at = (comp * PAIRS + pair) * LANES
            rows = [
                spectrum[part * NX : (part + 1) * NX, at : at + LANES] * masks[part // 2]
                for part in range(4)
            ]
            columns.append(jnp.concatenate(rows, 0).astype(jnp.bfloat16))
    return jnp.concatenate(columns, 1)


def combine_coils(arrived, factors, yi, zi):
    rows = product(yi, arrived).astype(jnp.bfloat16)
    half = 2 * NY
    places = range(0, arrived.shape[1], LANES)
    stacked = [
        jnp.concatenate([rows[:half, at : at + LANES], rows[half:, at : at + LANES]], 1)
        for at in places
    ]
    depth = product(jnp.concatenate(stacked, 0), zi)
    images = []
    for comp in range(len(places) // PAIRS):
        straight = turned = None
        for coil in range(COILS):
            at = (comp * PAIRS + coil // 2) * half
            image = depth[at : at + half, coil % 2 * LANES : (coil % 2 + 1) * LANES]
            real_map, turn_map = factors[coil]
            straight = real_map * image if coil == 0 else straight + real_map * image
            turned = turn_map * image if coil == 0 else turned + turn_map * image
        images.append(straight + swap_halves(turned))
    return images


def spread_out(images, factors, zf, yf):
    half = 2 * NY
    stacked = []
    for image in images:
        turned = swap_halves(image)
        spread = [
            (real_map * image + turn_map * turned).astype(jnp.bfloat16)
            for real_map, turn_map in factors
        ]
        stacked += [jnp.concatenate(spread[2 * pair : 2 * pair + 2], 1) for pair in range(PAIRS)]
    depth = product(jnp.concatenate(stacked, 0), zf).astype(jnp.bfloat16)
    columns = [
        jnp.concatenate([depth[at : at + half, :LANES], depth[at : at + half, LANES:]], 0)
        for at in range(0, depth.shape[0], half)
    ]
    return product(yf, jnp.concatenate(columns, 1)).astype(jnp.bfloat16)


def fold_rows(values):
    rows = values.sum(0, keepdims=True)
    return sum(rows[:, at : at + LANES] for at in range(0, rows.shape[1], LANES))


def row_of(one, other):
    return fold_rows(one.astype(jnp.float32) * other.astype(jnp.float32))


def group_step(sums):
    totals = sums[0:2].sum(1, keepdims=True)
    bb, data = totals[0:1], totals[1:2]
    usable = jnp.logical_and(bb > 0.0, data > 0.0)
    return jnp.where(usable, 0.5 * data, 1.0) / jnp.where(usable, bb, 1.0)


def final_scales(sums):
    totals = sums.sum(1, keepdims=True)
    bb, bq, qq, mixed, square = (totals[place : place + 1] for place in range(5))
    step_one = bb / bq
    norm_next = bb - 2.0 * step_one * bq + step_one * step_one * qq
    more = 1.0 + norm_next / bb
    curve = more * more * bq + 2.0 * more * step_one * mixed + step_one * step_one * square
    step_two = norm_next / curve
    return step_one + step_two * more, step_two * step_one


def first_kernel(
    kspace_at, sampling_at, order_at, xi_at, out, sum_out, kspace, sampling, order, xi, sems
):
    copies = [pltpu.make_async_copy(order_at, order, sems.at[0])]
    copies.append(pltpu.make_async_copy(sampling_at, sampling, sems.at[1]))
    for comp in range(kspace.shape[0]):
        copies.append(pltpu.make_async_copy(kspace_at.at[comp], kspace.at[comp], sems.at[2 + comp]))
    copies.append(pltpu.make_async_copy(xi_at, xi, sems.at[2 + kspace.shape[0]]))
    for copy in copies:
        copy.start()
    copies[0].wait()
    copies[1].wait()
    columns = []
    for comp in range(kspace.shape[0]):
        copies[2 + comp].wait()
        columns.append(first_masked(kspace[comp], sampling[comp], order[...]))
    copies[-1].wait()
    masked = jnp.concatenate(columns, 1)
    out[...] = product(xi[...], masked).astype(jnp.bfloat16)
    sum_out[...] = row_of(masked, masked)


def kspace_kernel(portion, sampling, xf, xi, out, masked_out, sum_out):
    masked = masked_spectrum(portion[...], sampling[...], xf[...])
    masked_out[...] = masked
    sum_out[...] = row_of(masked, masked)
    out[...] = product(xi[...], masked).astype(jnp.bfloat16)


def kspace_last_kernel(portion, sampling, xf, xi, masked_b, group, here, bq, qq, out, sums_out):
    masked = masked_spectrum(portion[...], sampling[...], xf[...])
    out[...] = product(xi[...], masked).astype(jnp.bfloat16)
    inverse_step = 1.0 / group_step(group[...])
    earlier = masked_b[...].astype(jnp.float32)
    change = (masked.astype(jnp.float32) - earlier) * inverse_step
    sums_out[0:1] = here[0:1]
    sums_out[1:2] = bq[...]
    sums_out[2:3] = qq[...]
    sums_out[3:4] = row_of(earlier, change)
    sums_out[4:5] = row_of(change, change)
    sums_out[5:8] = jnp.zeros((3, LANES), jnp.float32)


def image_kernel(arrived, coils, yi, zi, zf, yf, data, image_out, sums_out, out):
    factors = [coil_factors(coils[coil]) for coil in range(COILS)]
    images = combine_coils(arrived[...], factors, yi[...], zi[...])
    for comp, image in enumerate(images):
        image_out[comp] = image
    sums_out[0:1] = sum(row_of(image, image) for image in images)
    sums_out[1:2] = data[...]
    sums_out[2:8] = jnp.zeros((6, LANES), jnp.float32)
    out[...] = spread_out(images, factors, zf[...], yf[...])


def image_next_kernel(arrived, coils, yi, zi, zf, yf, b, group, image_out, sum_out, out):
    factors = [coil_factors(coils[coil]) for coil in range(COILS)]
    images = combine_coils(arrived[...], factors, yi[...], zi[...])
    for comp, image in enumerate(images):
        image_out[comp] = image
    sum_out[...] = sum(row_of(image, image) for image in images)
    step = group_step(group[...])
    images = [b[comp] - step * image for comp, image in enumerate(images)]
    out[...] = spread_out(images, factors, zf[...], yf[...])


def last_kernel(arrived, coils, yi, zi, b, q, group, sums, coefficients, residual):
    factors = [coil_factors(coils[coil]) for coil in range(COILS)]
    images = combine_coils(arrived[...], factors, yi[...], zi[...])
    along_b, along_q = final_scales(sums[...])
    along_t = along_q / group_step(group[...])
    for comp, image in enumerate(images):
        coefficients[comp] = along_b * b[comp] - along_q * q[comp]
        residual[comp] = b[comp] - along_b * q[comp] + along_t * (q[comp] - image)


def call(body, operands, shapes, flops, space=pltpu.VMEM, scratch=(), mebibytes=32):
    held = sum(math.prod(o.shape) * o.dtype.itemsize for o in operands)
    held += sum(math.prod(s.shape) * s.dtype.itemsize for s in shapes)
    return pl.pallas_call(
        body,
        out_shape=shapes,
        in_specs=[pl.BlockSpec(memory_space=space)] * len(operands),
        out_specs=[pl.BlockSpec(memory_space=pltpu.VMEM)] * len(shapes),
        scratch_shapes=scratch,
        compiler_params=pltpu.CompilerParams(vmem_limit_bytes=mebibytes * 1024 * 1024),
        cost_estimate=pl.CostEstimate(flops=flops, bytes_accessed=held, transcendentals=0),
    )(*operands)


def exchange(values):
    return lax.all_to_all(values, "slab", split_axis=0, concat_axis=0, tiled=True)


def exclusive(axis, flips):
    return [(place, place ^ flips) for place in range(lax.axis_size(axis))]


def sum_over(values, axis, low, count):
    terms = [values]
    terms += [lax.ppermute(values, axis, exclusive(axis, flips * low)) for flips in range(1, count)]
    while len(terms) > 1:
        terms = [one + other for one, other in zip(terms[::2], terms[1::2])]
    return terms[0]


def total_of(values, steps):
    for axis, low, count in steps:
        values = sum_over(values, axis, low, count)
    return values


def shards(kspace, sensitivities, sampling):
    comps = kspace.shape[0]
    tables = {name: jnp.asarray(value) for name, value in make_tables().items()}
    coils = sensitivities.reshape(COILS, 2, NY, LANES).transpose(0, 2, 1, 3)
    coils = coils.reshape(COILS, 2 * NY, LANES)
    width = comps * PAIRS * LANES
    sent_shape = jax.ShapeDtypeStruct((4 * NX, width), jnp.bfloat16)
    image_shape = jax.ShapeDtypeStruct((comps, 2 * NY, LANES), jnp.float32)
    sum_shape = jax.ShapeDtypeStruct((1, LANES), jnp.float32)
    sums_shape = jax.ShapeDtypeStruct((8, LANES), jnp.float32)
    square = 2 * (4 * NX) * (4 * NX) * width

    def image_step(body, arrived, earlier, sums):
        operands = [arrived, coils] + [tables[name] for name in ("yi", "zi", "zf", "yf")]
        return call(body, operands + earlier, [image_shape, sums, sent_shape], 3 * square)

    first = [kspace, sampling, tables["order"], tables["xi"]]
    scratch = [pltpu.VMEM(array.shape, array.dtype) for array in first]
    scratch.append(pltpu.SemaphoreType.DMA((3 + comps,)))
    sent, data = call(first_kernel, first, [sent_shape, sum_shape], 2 * square, pltpu.HBM, scratch, 58)
    b, here, sent = image_step(image_kernel, exchange(sent), [data], sums_shape)
    arrived, group = exchange(sent), total_of(here, GROUP_STEPS[:2])
    arrived, group = lax.optimization_barrier((arrived, group))
    operands = [arrived, sampling, tables["xf"], tables["xi"]]
    sent, masked_b, bq = call(
        kspace_kernel, operands, [sent_shape, sent_shape, sum_shape], 2 * square
    )
    sent, group = lax.optimization_barrier((sent, group))
    group = total_of(group, GROUP_STEPS[2:])
    q, qq, sent = image_step(image_next_kernel, exchange(sent), [b, group], sum_shape)
    operands = [exchange(sent), sampling, tables["xf"], tables["xi"], masked_b, group, here, bq, qq]
    sent, sums = call(kspace_last_kernel, operands, [sent_shape, sums_shape], 2 * square)
    arrived = exchange(sent)
    operands = [arrived, coils, tables["yi"], tables["zi"], b, q, group, total_of(sums, STEPS)]
    outputs = call(last_kernel, operands, [image_shape] * 2, 2 * square)
    return tuple(
        output.reshape(comps, NY, 2, LANES).transpose(0, 2, 1, 3).reshape(comps, 2, -1)
        for output in outputs
    )


def solution(mesh):
    in_specs = (P("comp", None, None, "slab"), P(None, "slab", None), P("comp", None, "slab"))
    out_specs = (P("comp", "slab", None), P("comp", "slab", None))
    return jax.shard_map(shards, mesh=mesh, in_specs=in_specs, out_specs=out_specs, check_vma=False)
```

```python
import math

import jax
import jax.numpy as jnp
import numpy as np
from jax import lax
from jax.experimental import pallas as pl
from jax.experimental.pallas import tpu as pltpu
from jax.sharding import PartitionSpec as P

NX = 128
NY = 128
NZ = 64
COILS = 4
PAIRS = COILS // 2
LANES = 2 * NZ
GROUP_STEPS = (("slab", 1, 4), ("slab", 4, 4), ("slab", 16, 4))
STEPS = (("comp", 1, 4),) + GROUP_STEPS


def fourier_blocks(length, orientation):
    positions = np.arange(length)
    angles = (positions[:, None] * positions[None, :] % length) * (2.0 * math.pi / length)
    scaling = 1.0 / math.sqrt(length)
    real_part = np.cos(angles) * scaling
    imaginary = orientation * np.sin(angles) * scaling
    top_rows = np.stack([real_part, -imaginary], 1)
    low_rows = np.stack([imaginary, real_part], 1)
    return np.stack([top_rows, low_rows], 0).astype(np.float32)


def table(spec, *factors, shape):
    return np.einsum(spec, *factors).reshape(shape).astype(jnp.bfloat16)


def make_tables():
    two = np.eye(2, dtype=np.float32)
    slabs = NX // 2
    zf, zi = fourier_blocks(NZ, -1.0), fourier_blocks(NZ, 1.0)
    yf, yi = fourier_blocks(NY, -1.0), fourier_blocks(NY, 1.0)
    xf = fourier_blocks(NX, -1.0).reshape(2, NX, 2, slabs, 2)
    xi = fourier_blocks(NX, 1.0).reshape(2, slabs, 2, 2, NX)
    return {
        "zf": table("akbj,cd->cbjadk", zf, two, shape=(4 * NZ, 4 * NZ)),
        "zi": table("akbj,cd->bcjdak", zi, two, shape=(4 * NZ, 4 * NZ)),
        "yf": table("akbj,cd->kcabjd", yf, two, shape=(4 * NY, 4 * NY)),
        "yi": table("akbj,cd->akcjdb", yi, two, shape=(4 * NY, 4 * NY)),
        "xf": table("akbst,cd->caksdtb", xf, two, shape=(4 * NX, 4 * NX)),
        "xi": table("astbk,cd->sctadbk", xi, two, shape=(4 * NX, 4 * NX)),
        "order": table(
            "ab,ef,gh->aegfbh", two, two, np.eye(NZ, dtype=np.float32), shape=(4 * NZ, 4 * NZ)
        ),
    }


def product(left, right):
    return jnp.dot(left, right, preferred_element_type=jnp.float32)


def swap_halves(values):
    return pltpu.roll(values, NZ, values.ndim - 1)


def low_half(shape):
    return lax.broadcasted_iota(jnp.int32, shape, len(shape) - 1) < NZ


def masks_of(sampling):
    pattern = sampling.astype(jnp.float32)
    other = swap_halves(pattern)
    low = low_half(pattern.shape)
    return jnp.where(low, pattern, other), jnp.where(low, other, pattern)


def coil_factors(maps):
    other = swap_halves(maps)
    low = low_half(maps.shape)
    return jnp.where(low, maps, other), jnp.where(low, -other, maps)


def first_masked(kspace, sampling, order):
    masks = masks_of(sampling)
    stacked = [
        jnp.concatenate(
            [kspace[coil][:, place * LANES : (place + 1) * LANES] for coil in (2 * pair, 2 * pair + 1)], 1
        )
        for pair in range(PAIRS)
        for place in range(2)
    ]
    ordered = product(jnp.concatenate(stacked, 0), order)
    columns = []
    for pair in range(PAIRS):
        rows = []
        for place in range(2):
            at = (2 * pair + place) * NX
            rows += [
                ordered[at : at + NX, part * LANES : (part + 1) * LANES] * masks[place]
                for part in range(2)
            ]
        columns.append(jnp.concatenate(rows, 0).astype(jnp.bfloat16))
    return jnp.concatenate(columns, 1)


def masked_spectrum(portion, sampling, xf):
    spectrum = product(xf, portion)
    columns = []
    for comp in range(sampling.shape[0]):
        masks = masks_of(sampling[comp])
        for pair in range(PAIRS):
            at = (comp * PAIRS + pair) * LANES
            rows = [
                spectrum[part * NX : (part + 1) * NX, at : at + LANES] * masks[part // 2]
                for part in range(4)
            ]
            columns.append(jnp.concatenate(rows, 0).astype(jnp.bfloat16))
    return jnp.concatenate(columns, 1)


def combine_coils(arrived, factors, yi, zi):
    rows = product(yi, arrived).astype(jnp.bfloat16)
    half = 2 * NY
    places = range(0, arrived.shape[1], LANES)
    stacked = [
        jnp.concatenate([rows[:half, at : at + LANES], rows[half:, at : at + LANES]], 1)
        for at in places
    ]
    depth = product(jnp.concatenate(stacked, 0), zi)
    images = []
    for comp in range(len(places) // PAIRS):
        straight = turned = None
        for coil in range(COILS):
            at = (comp * PAIRS + coil // 2) * half
            image = depth[at : at + half, coil % 2 * LANES : (coil % 2 + 1) * LANES]
            real_map, turn_map = factors[coil]
            straight = real_map * image if coil == 0 else straight + real_map * image
            turned = turn_map * image if coil == 0 else turned + turn_map * image
        images.append(straight + swap_halves(turned))
    return images


def spread_out(images, factors, zf, yf):
    half = 2 * NY
    stacked = []
    for image in images:
        turned = swap_halves(image)
        spread = [
            (real_map * image + turn_map * turned).astype(jnp.bfloat16)
            for real_map, turn_map in factors
        ]
        stacked += [jnp.concatenate(spread[2 * pair : 2 * pair + 2], 1) for pair in range(PAIRS)]
    depth = product(jnp.concatenate(stacked, 0), zf).astype(jnp.bfloat16)
    columns = [
        jnp.concatenate([depth[at : at + half, :LANES], depth[at : at + half, LANES:]], 0)
        for at in range(0, depth.shape[0], half)
    ]
    return product(yf, jnp.concatenate(columns, 1)).astype(jnp.bfloat16)


def fold_rows(values):
    rows = values.sum(0, keepdims=True)
    return sum(rows[:, at : at + LANES] for at in range(0, rows.shape[1], LANES))


def row_of(one, other):
    return fold_rows(one.astype(jnp.float32) * other.astype(jnp.float32))


def group_step(sums):
    totals = sums[0:2].sum(1, keepdims=True)
    bb, data = totals[0:1], totals[1:2]
    usable = jnp.logical_and(bb > 0.0, data > 0.0)
    return jnp.where(usable, 0.5 * data, 1.0) / jnp.where(usable, bb, 1.0)


def final_scales(sums):
    totals = sums.sum(1, keepdims=True)
    bb, bq, qq, mixed, square = (totals[place : place + 1] for place in range(5))
    step_one = bb / bq
    norm_next = bb - 2.0 * step_one * bq + step_one * step_one * qq
    more = 1.0 + norm_next / bb
    curve = more * more * bq + 2.0 * more * step_one * mixed + step_one * step_one * square
    step_two = norm_next / curve
    return step_one + step_two * more, step_two * step_one


def first_kernel(
    kspace_at, sampling_at, order_at, xi_at, out, sum_out, kspace, sampling, order, xi, sems
):
    copies = [pltpu.make_async_copy(order_at, order, sems.at[0])]
    copies.append(pltpu.make_async_copy(sampling_at, sampling, sems.at[1]))
    for comp in range(kspace.shape[0]):
        copies.append(pltpu.make_async_copy(kspace_at.at[comp], kspace.at[comp], sems.at[2 + comp]))
    copies.append(pltpu.make_async_copy(xi_at, xi, sems.at[2 + kspace.shape[0]]))
    for copy in copies:
        copy.start()
    copies[0].wait()
    copies[1].wait()
    columns = []
    for comp in range(kspace.shape[0]):
        copies[2 + comp].wait()
        columns.append(first_masked(kspace[comp], sampling[comp], order[...]))
    copies[-1].wait()
    masked = jnp.concatenate(columns, 1)
    out[...] = product(xi[...], masked).astype(jnp.bfloat16)
    sum_out[...] = row_of(masked, masked)


def kspace_kernel(portion, sampling, xf, xi, out, masked_at, sum_out, kept, sem):
    masked = masked_spectrum(portion[...], sampling[...], xf[...])
    kept[...] = masked
    copy = pltpu.make_async_copy(kept, masked_at, sem)
    copy.start()
    out[...] = product(xi[...], masked).astype(jnp.bfloat16)
    sum_out[...] = row_of(masked, masked)
    copy.wait()


def kspace_last_kernel(
    portion, sampling, xf, xi, masked_at, group, here, bq, qq, out, sums_out, masked_b, sem
):
    copy = pltpu.make_async_copy(masked_at, masked_b, sem)
    copy.start()
    masked = masked_spectrum(portion[...], sampling[...], xf[...])
    out[...] = product(xi[...], masked).astype(jnp.bfloat16)
    inverse_step = 1.0 / group_step(group[...])
    copy.wait()
    earlier = masked_b[...].astype(jnp.float32)
    change = (masked.astype(jnp.float32) - earlier) * inverse_step
    sums_out[0:1] = here[0:1]
    sums_out[1:2] = bq[...]
    sums_out[2:3] = qq[...]
    sums_out[3:4] = row_of(earlier, change)
    sums_out[4:5] = row_of(change, change)
    sums_out[5:8] = jnp.zeros((3, LANES), jnp.float32)


def image_kernel(arrived, coils, yi, zi, zf, yf, data, image_at, sums_out, out, kept, sem):
    factors = [coil_factors(coils[coil]) for coil in range(COILS)]
    images = combine_coils(arrived[...], factors, yi[...], zi[...])
    for comp, image in enumerate(images):
        kept[comp] = image
    copy = pltpu.make_async_copy(kept, image_at, sem)
    copy.start()
    sums_out[0:1] = sum(row_of(image, image) for image in images)
    sums_out[1:2] = data[...]
    sums_out[2:8] = jnp.zeros((6, LANES), jnp.float32)
    out[...] = spread_out(images, factors, zf[...], yf[...])
    copy.wait()


def image_next_kernel(
    arrived, coils, yi, zi, zf, yf, b_at, group, image_at, sum_out, out, kept, sem, b, b_sem
):
    b_copy = pltpu.make_async_copy(b_at, b, b_sem)
    b_copy.start()
    factors = [coil_factors(coils[coil]) for coil in range(COILS)]
    images = combine_coils(arrived[...], factors, yi[...], zi[...])
    for comp, image in enumerate(images):
        kept[comp] = image
    copy = pltpu.make_async_copy(kept, image_at, sem)
    copy.start()
    sum_out[...] = sum(row_of(image, image) for image in images)
    b_copy.wait()
    step = group_step(group[...])
    images = [b[comp] - step * image for comp, image in enumerate(images)]
    out[...] = spread_out(images, factors, zf[...], yf[...])
    copy.wait()


def last_kernel(
    arrived, coils, yi, zi, b_at, q_at, group, sums, coefficients, residual, b, q, b_sem, q_sem
):
    copies = [pltpu.make_async_copy(b_at, b, b_sem), pltpu.make_async_copy(q_at, q, q_sem)]
    for copy in copies:
        copy.start()
    factors = [coil_factors(coils[coil]) for coil in range(COILS)]
    images = combine_coils(arrived[...], factors, yi[...], zi[...])
    along_b, along_q = final_scales(sums[...])
    along_t = along_q / group_step(group[...])
    for copy in copies:
        copy.wait()
    for comp, image in enumerate(images):
        coefficients[comp] = along_b * b[comp] - along_q * q[comp]
        residual[comp] = b[comp] - along_b * q[comp] + along_t * (q[comp] - image)


def call(body, operands, shapes, flops, far=(), far_out=(), scratch=(), mebibytes=32):
    held = sum(math.prod(o.shape) * o.dtype.itemsize for o in operands)
    held += sum(math.prod(s.shape) * s.dtype.itemsize for s in shapes)
    operands = [
        pltpu.with_memory_space_constraint(operand, pltpu.HBM) if place in far else operand
        for place, operand in enumerate(operands)
    ]
    return pl.pallas_call(
        body,
        out_shape=[
            pltpu.HBM(shape.shape, shape.dtype) if place in far_out else shape
            for place, shape in enumerate(shapes)
        ],
        in_specs=[
            pl.BlockSpec(memory_space=pltpu.HBM if place in far else pltpu.VMEM)
            for place in range(len(operands))
        ],
        out_specs=[
            pl.BlockSpec(memory_space=pltpu.HBM if place in far_out else pltpu.VMEM)
            for place in range(len(shapes))
        ],
        scratch_shapes=scratch,
        compiler_params=pltpu.CompilerParams(vmem_limit_bytes=mebibytes * 1024 * 1024),
        cost_estimate=pl.CostEstimate(flops=flops, bytes_accessed=held, transcendentals=0),
    )(*operands)


def exchange(values):
    return lax.all_to_all(values, "slab", split_axis=0, concat_axis=0, tiled=True)


def exclusive(axis, flips):
    return [(place, place ^ flips) for place in range(lax.axis_size(axis))]


def sum_over(values, axis, low, count):
    terms = [values]
    terms += [lax.ppermute(values, axis, exclusive(axis, flips * low)) for flips in range(1, count)]
    while len(terms) > 1:
        terms = [one + other for one, other in zip(terms[::2], terms[1::2])]
    return terms[0]


def total_of(values, steps):
    for axis, low, count in steps:
        values = sum_over(values, axis, low, count)
    return values


def shards(kspace, sensitivities, sampling):
    comps = kspace.shape[0]
    tables = {name: jnp.asarray(value) for name, value in make_tables().items()}
    coils = sensitivities.reshape(COILS, 2, NY, LANES).transpose(0, 2, 1, 3)
    coils = coils.reshape(COILS, 2 * NY, LANES)
    width = comps * PAIRS * LANES
    sent_shape = jax.ShapeDtypeStruct((4 * NX, width), jnp.bfloat16)
    image_shape = jax.ShapeDtypeStruct((comps, 2 * NY, LANES), jnp.float32)
    sum_shape = jax.ShapeDtypeStruct((1, LANES), jnp.float32)
    sums_shape = jax.ShapeDtypeStruct((8, LANES), jnp.float32)
    square = 2 * (4 * NX) * (4 * NX) * width

    sem = pltpu.SemaphoreType.DMA
    image_kept = pltpu.VMEM(image_shape.shape, jnp.float32)
    sent_kept = pltpu.VMEM(sent_shape.shape, jnp.bfloat16)

    def image_step(body, arrived, earlier, sums, far, scratch):
        operands = [arrived, coils] + [tables[name] for name in ("yi", "zi", "zf", "yf")]
        shapes = [image_shape, sums, sent_shape]
        return call(body, operands + earlier, shapes, 3 * square, far, (0,), scratch)

    first = [kspace, sampling, tables["order"], tables["xi"]]
    scratch = [pltpu.VMEM(array.shape, array.dtype) for array in first]
    scratch.append(pltpu.SemaphoreType.DMA((3 + comps,)))
    sent, data = call(
        first_kernel, first, [sent_shape, sum_shape], 2 * square, range(4), (), scratch, 58
    )
    b, here, sent = image_step(image_kernel, exchange(sent), [data], sums_shape, (), [image_kept, sem])
    arrived, group = exchange(sent), total_of(here, GROUP_STEPS[:2])
    arrived, group = lax.optimization_barrier((arrived, group))
    operands = [arrived, sampling, tables["xf"], tables["xi"]]
    shapes = [sent_shape, sent_shape, sum_shape]
    sent, masked_b, bq = call(
        kspace_kernel, operands, shapes, 2 * square, (), (1,), [sent_kept, sem]
    )
    sent, group = lax.optimization_barrier((sent, group))
    group = total_of(group, GROUP_STEPS[2:])
    scratch = [image_kept, sem, image_kept, sem]
    q, qq, sent = image_step(image_next_kernel, exchange(sent), [b, group], sum_shape, (6,), scratch)
    operands = [exchange(sent), sampling, tables["xf"], tables["xi"], masked_b, group, here, bq, qq]
    sent, sums = call(kspace_last_kernel, operands, [sent_shape, sums_shape], 2 * square, (4,), (), [sent_kept, sem])
    arrived = exchange(sent)
    operands = [arrived, coils, tables["yi"], tables["zi"], b, q, group, total_of(sums, STEPS)]
    scratch = [image_kept, image_kept, sem, sem]
    outputs = call(last_kernel, operands, [image_shape] * 2, 2 * square, (4, 5), (), scratch)
    return tuple(
        output.reshape(comps, NY, 2, LANES).transpose(0, 2, 1, 3).reshape(comps, 2, -1)
        for output in outputs
    )


def solution(mesh):
    in_specs = (P("comp", None, None, "slab"), P(None, "slab", None), P("comp", None, "slab"))
    out_specs = (P("comp", "slab", None), P("comp", "slab", None))
    return jax.shard_map(shards, mesh=mesh, in_specs=in_specs, out_specs=out_specs, check_vma=False)
```

```python
import math

import jax
import jax.numpy as jnp
import numpy as np
from jax import lax
from jax.experimental import pallas as pl
from jax.experimental.pallas import tpu as pltpu
from jax.sharding import PartitionSpec as P

NX = 128
NY = 128
NZ = 64
COILS = 4
PAIRS = COILS // 2
LANES = 2 * NZ
GROUP_STEPS = (("slab", 1, 4), ("slab", 4, 4), ("slab", 16, 4))
STEPS = (("comp", 1, 4),) + GROUP_STEPS


def fourier_blocks(length, orientation):
    positions = np.arange(length)
    angles = (positions[:, None] * positions[None, :] % length) * (2.0 * math.pi / length)
    scaling = 1.0 / math.sqrt(length)
    real_part = np.cos(angles) * scaling
    imaginary = orientation * np.sin(angles) * scaling
    top_rows = np.stack([real_part, -imaginary], 1)
    low_rows = np.stack([imaginary, real_part], 1)
    return np.stack([top_rows, low_rows], 0).astype(np.float32)


def table(spec, *factors, shape):
    return np.einsum(spec, *factors).reshape(shape).astype(jnp.bfloat16)


def make_tables():
    two = np.eye(2, dtype=np.float32)
    slabs = NX // 2
    zf, zi = fourier_blocks(NZ, -1.0), fourier_blocks(NZ, 1.0)
    yf, yi = fourier_blocks(NY, -1.0), fourier_blocks(NY, 1.0)
    xf = fourier_blocks(NX, -1.0).reshape(2, NX, 2, slabs, 2)
    xi = fourier_blocks(NX, 1.0).reshape(2, slabs, 2, 2, NX)
    return {
        "zf": table("akbj,cd->cbjadk", zf, two, shape=(4 * NZ, 4 * NZ)),
        "zi": table("akbj,cd->bcjdak", zi, two, shape=(4 * NZ, 4 * NZ)),
        "yf": table("akbj,cd->kcabjd", yf, two, shape=(4 * NY, 4 * NY)),
        "yi": table("akbj,cd->akcjdb", yi, two, shape=(4 * NY, 4 * NY)),
        "xf": table("akbst,cd->caksdtb", xf, two, shape=(4 * NX, 4 * NX)),
        "xi": table("astbk,cd->sctadbk", xi, two, shape=(4 * NX, 4 * NX)),
        "order": table(
            "ab,ef,gh->aegfbh", two, two, np.eye(NZ, dtype=np.float32), shape=(4 * NZ, 4 * NZ)
        ),
    }


def product(left, right):
    return jnp.dot(left, right, preferred_element_type=jnp.float32)


def swap_halves(values):
    return pltpu.roll(values, NZ, values.ndim - 1)


def low_half(shape):
    return lax.broadcasted_iota(jnp.int32, shape, len(shape) - 1) < NZ


def masks_of(sampling):
    pattern = sampling.astype(jnp.float32)
    other = swap_halves(pattern)
    low = low_half(pattern.shape)
    return jnp.where(low, pattern, other), jnp.where(low, other, pattern)


def coil_factors(maps):
    other = swap_halves(maps)
    low = low_half(maps.shape)
    return jnp.where(low, maps, other), jnp.where(low, -other, maps)


def first_masked(kspace, sampling, order):
    masks = masks_of(sampling)
    stacked = [
        jnp.concatenate(
            [kspace[coil][:, place * LANES : (place + 1) * LANES] for coil in (2 * pair, 2 * pair + 1)], 1
        )
        for pair in range(PAIRS)
        for place in range(2)
    ]
    ordered = product(jnp.concatenate(stacked, 0), order)
    columns = []
    for pair in range(PAIRS):
        rows = []
        for place in range(2):
            at = (2 * pair + place) * NX
            rows += [
                ordered[at : at + NX, part * LANES : (part + 1) * LANES] * masks[place]
                for part in range(2)
            ]
        columns.append(jnp.concatenate(rows, 0).astype(jnp.bfloat16))
    return jnp.concatenate(columns, 1)


def masked_spectrum(portion, sampling, xf):
    spectrum = product(xf, portion)
    columns = []
    for comp in range(sampling.shape[0]):
        masks = masks_of(sampling[comp])
        for pair in range(PAIRS):
            at = (comp * PAIRS + pair) * LANES
            rows = [
                spectrum[part * NX : (part + 1) * NX, at : at + LANES] * masks[part // 2]
                for part in range(4)
            ]
            columns.append(jnp.concatenate(rows, 0).astype(jnp.bfloat16))
    return jnp.concatenate(columns, 1)


def combine_coils(arrived, factors, yi, zi):
    rows = product(yi, arrived).astype(jnp.bfloat16)
    half = 2 * NY
    places = range(0, arrived.shape[1], LANES)
    stacked = [
        jnp.concatenate([rows[:half, at : at + LANES], rows[half:, at : at + LANES]], 1)
        for at in places
    ]
    depth = product(jnp.concatenate(stacked, 0), zi)
    images = []
    for comp in range(len(places) // PAIRS):
        straight = turned = None
        for coil in range(COILS):
            at = (comp * PAIRS + coil // 2) * half
            image = depth[at : at + half, coil % 2 * LANES : (coil % 2 + 1) * LANES]
            real_map, turn_map = factors[coil]
            straight = real_map * image if coil == 0 else straight + real_map * image
            turned = turn_map * image if coil == 0 else turned + turn_map * image
        images.append(straight + swap_halves(turned))
    return images


def spread_out(images, factors, zf, yf):
    half = 2 * NY
    stacked = []
    for image in images:
        turned = swap_halves(image)
        spread = [
            (real_map * image + turn_map * turned).astype(jnp.bfloat16)
            for real_map, turn_map in factors
        ]
        stacked += [jnp.concatenate(spread[2 * pair : 2 * pair + 2], 1) for pair in range(PAIRS)]
    depth = product(jnp.concatenate(stacked, 0), zf).astype(jnp.bfloat16)
    columns = [
        jnp.concatenate([depth[at : at + half, :LANES], depth[at : at + half, LANES:]], 0)
        for at in range(0, depth.shape[0], half)
    ]
    return product(yf, jnp.concatenate(columns, 1)).astype(jnp.bfloat16)


def fold_rows(values):
    rows = values.sum(0, keepdims=True)
    return sum(rows[:, at : at + LANES] for at in range(0, rows.shape[1], LANES))


def row_of(one, other):
    return fold_rows(one.astype(jnp.float32) * other.astype(jnp.float32))


def group_step(sums):
    totals = sums[0:2].sum(1, keepdims=True)
    bb, data = totals[0:1], totals[1:2]
    usable = jnp.logical_and(bb > 0.0, data > 0.0)
    return jnp.where(usable, 0.5 * data, 1.0) / jnp.where(usable, bb, 1.0)


def final_scales(sums):
    totals = sums.sum(1, keepdims=True)
    bb, bq, qq, mixed, square = (totals[place : place + 1] for place in range(5))
    step_one = bb / bq
    norm_next = bb - 2.0 * step_one * bq + step_one * step_one * qq
    more = 1.0 + norm_next / bb
    curve = more * more * bq + 2.0 * more * step_one * mixed + step_one * step_one * square
    step_two = norm_next / curve
    return step_one + step_two * more, step_two * step_one


def first_kernel(
    kspace_at, sampling_at, order_at, xi_at, out, sum_out, kspace, sampling, order, xi, sems
):
    copies = [pltpu.make_async_copy(order_at, order, sems.at[0])]
    copies.append(pltpu.make_async_copy(sampling_at, sampling, sems.at[1]))
    for comp in range(kspace.shape[0]):
        copies.append(pltpu.make_async_copy(kspace_at.at[comp], kspace.at[comp], sems.at[2 + comp]))
    copies.append(pltpu.make_async_copy(xi_at, xi, sems.at[2 + kspace.shape[0]]))
    for copy in copies:
        copy.start()
    copies[0].wait()
    copies[1].wait()
    columns = []
    for comp in range(kspace.shape[0]):
        copies[2 + comp].wait()
        columns.append(first_masked(kspace[comp], sampling[comp], order[...]))
    copies[-1].wait()
    masked = jnp.concatenate(columns, 1)
    out[...] = product(xi[...], masked).astype(jnp.bfloat16)
    sum_out[...] = row_of(masked, masked)


def kspace_kernel(portion, sampling, xf, xi, out, sum_out):
    masked = masked_spectrum(portion[...], sampling[...], xf[...])
    sum_out[...] = row_of(masked, masked)
    out[...] = product(xi[...], masked).astype(jnp.bfloat16)


def kspace_last_kernel(portion, sampling, xf, xi, group, here, bq, image_sums, out, sums_out):
    masked = masked_spectrum(portion[...], sampling[...], xf[...])
    out[...] = product(xi[...], masked).astype(jnp.bfloat16)
    inverse_step = 1.0 / group_step(group[...])
    qp = image_sums[1:2]
    sums_out[0:1] = here[0:1]
    sums_out[1:2] = bq[...]
    sums_out[2:3] = image_sums[0:1]
    sums_out[3:4] = (qp - bq[...]) * inverse_step
    sums_out[4:5] = (bq[...] - 2.0 * qp + row_of(masked, masked)) * (inverse_step * inverse_step)
    sums_out[5:8] = jnp.zeros((3, LANES), jnp.float32)


def image_kernel(arrived, coils, yi, zi, zf, yf, data, image_out, sums_out, out):
    factors = [coil_factors(coils[coil]) for coil in range(COILS)]
    images = combine_coils(arrived[...], factors, yi[...], zi[...])
    for comp, image in enumerate(images):
        image_out[comp] = image
    sums_out[0:1] = sum(row_of(image, image) for image in images)
    sums_out[1:2] = data[...]
    sums_out[2:8] = jnp.zeros((6, LANES), jnp.float32)
    out[...] = spread_out(images, factors, zf[...], yf[...])


def image_next_kernel(arrived, coils, yi, zi, zf, yf, b, group, image_out, sums_out, out):
    factors = [coil_factors(coils[coil]) for coil in range(COILS)]
    images = combine_coils(arrived[...], factors, yi[...], zi[...])
    for comp, image in enumerate(images):
        image_out[comp] = image
    step = group_step(group[...])
    moved = [b[comp] - step * image for comp, image in enumerate(images)]
    sums_out[0:1] = sum(row_of(image, image) for image in images)
    sums_out[1:2] = sum(row_of(image, other) for image, other in zip(images, moved))
    sums_out[2:8] = jnp.zeros((6, LANES), jnp.float32)
    out[...] = spread_out(moved, factors, zf[...], yf[...])


def last_kernel(arrived, coils, yi, zi, b, q, group, sums, coefficients, residual):
    factors = [coil_factors(coils[coil]) for coil in range(COILS)]
    images = combine_coils(arrived[...], factors, yi[...], zi[...])
    along_b, along_q = final_scales(sums[...])
    along_t = along_q / group_step(group[...])
    for comp, image in enumerate(images):
        coefficients[comp] = along_b * b[comp] - along_q * q[comp]
        residual[comp] = b[comp] - along_b * q[comp] + along_t * (q[comp] - image)


def call(body, operands, shapes, flops, space=pltpu.VMEM, scratch=(), mebibytes=32):
    held = sum(math.prod(o.shape) * o.dtype.itemsize for o in operands)
    held += sum(math.prod(s.shape) * s.dtype.itemsize for s in shapes)
    return pl.pallas_call(
        body,
        out_shape=shapes,
        in_specs=[pl.BlockSpec(memory_space=space)] * len(operands),
        out_specs=[pl.BlockSpec(memory_space=pltpu.VMEM)] * len(shapes),
        scratch_shapes=scratch,
        compiler_params=pltpu.CompilerParams(vmem_limit_bytes=mebibytes * 1024 * 1024),
        cost_estimate=pl.CostEstimate(flops=flops, bytes_accessed=held, transcendentals=0),
    )(*operands)


def exchange(values):
    return lax.all_to_all(values, "slab", split_axis=0, concat_axis=0, tiled=True)


def exclusive(axis, flips):
    return [(place, place ^ flips) for place in range(lax.axis_size(axis))]


def sum_over(values, axis, low, count):
    terms = [values]
    terms += [lax.ppermute(values, axis, exclusive(axis, flips * low)) for flips in range(1, count)]
    while len(terms) > 1:
        terms = [one + other for one, other in zip(terms[::2], terms[1::2])]
    return terms[0]


def total_of(values, steps):
    for axis, low, count in steps:
        values = sum_over(values, axis, low, count)
    return values


def shards(kspace, sensitivities, sampling):
    comps = kspace.shape[0]
    tables = {name: jnp.asarray(value) for name, value in make_tables().items()}
    coils = sensitivities.reshape(COILS, 2, NY, LANES).transpose(0, 2, 1, 3)
    coils = coils.reshape(COILS, 2 * NY, LANES)
    width = comps * PAIRS * LANES
    sent_shape = jax.ShapeDtypeStruct((4 * NX, width), jnp.bfloat16)
    image_shape = jax.ShapeDtypeStruct((comps, 2 * NY, LANES), jnp.float32)
    sum_shape = jax.ShapeDtypeStruct((1, LANES), jnp.float32)
    sums_shape = jax.ShapeDtypeStruct((8, LANES), jnp.float32)
    square = 2 * (4 * NX) * (4 * NX) * width

    def image_step(body, arrived, earlier, sums):
        operands = [arrived, coils] + [tables[name] for name in ("yi", "zi", "zf", "yf")]
        return call(body, operands + earlier, [image_shape, sums, sent_shape], 3 * square)

    first = [kspace, sampling, tables["order"], tables["xi"]]
    scratch = [pltpu.VMEM(array.shape, array.dtype) for array in first]
    scratch.append(pltpu.SemaphoreType.DMA((3 + comps,)))
    sent, data = call(first_kernel, first, [sent_shape, sum_shape], 2 * square, pltpu.HBM, scratch, 58)
    b, here, sent = image_step(image_kernel, exchange(sent), [data], sums_shape)
    arrived, group = exchange(sent), total_of(here, GROUP_STEPS[:2])
    arrived, group = lax.optimization_barrier((arrived, group))
    operands = [arrived, sampling, tables["xf"], tables["xi"]]
    sent, bq = call(kspace_kernel, operands, [sent_shape, sum_shape], 2 * square)
    sent, group = lax.optimization_barrier((sent, group))
    group = total_of(group, GROUP_STEPS[2:])
    q, image_sums, sent = image_step(image_next_kernel, exchange(sent), [b, group], sums_shape)
    operands = [exchange(sent), sampling, tables["xf"], tables["xi"], group, here, bq, image_sums]
    sent, sums = call(kspace_last_kernel, operands, [sent_shape, sums_shape], 2 * square)
    arrived = exchange(sent)
    operands = [arrived, coils, tables["yi"], tables["zi"], b, q, group, total_of(sums, STEPS)]
    outputs = call(last_kernel, operands, [image_shape] * 2, 2 * square)
    return tuple(
        output.reshape(comps, NY, 2, LANES).transpose(0, 2, 1, 3).reshape(comps, 2, -1)
        for output in outputs
    )


def solution(mesh):
    in_specs = (P("comp", None, None, "slab"), P(None, "slab", None), P("comp", None, "slab"))
    out_specs = (P("comp", "slab", None), P("comp", "slab", None))
    return jax.shard_map(shards, mesh=mesh, in_specs=in_specs, out_specs=out_specs, check_vma=False)
```

```python
import math

import jax
import jax.numpy as jnp
import numpy as np
from jax import lax
from jax.experimental import pallas as pl
from jax.experimental.pallas import tpu as pltpu
from jax.sharding import PartitionSpec as P

NX = 128
NY = 128
NZ = 64
COILS = 4
PAIRS = COILS // 2
LANES = 2 * NZ
GROUP_STEPS = (("slab", 1, 4), ("slab", 4, 4), ("slab", 16, 4))
STEPS = (("comp", 1, 4),) + GROUP_STEPS


def fourier_blocks(length, orientation):
    positions = np.arange(length)
    angles = (positions[:, None] * positions[None, :] % length) * (2.0 * math.pi / length)
    scaling = 1.0 / math.sqrt(length)
    real_part = np.cos(angles) * scaling
    imaginary = orientation * np.sin(angles) * scaling
    top_rows = np.stack([real_part, -imaginary], 1)
    low_rows = np.stack([imaginary, real_part], 1)
    return np.stack([top_rows, low_rows], 0).astype(np.float32)


def table(spec, *factors, shape):
    return np.einsum(spec, *factors).reshape(shape).astype(jnp.bfloat16)


def make_tables():
    two = np.eye(2, dtype=np.float32)
    slabs = NX // 2
    zf, zi = fourier_blocks(NZ, -1.0), fourier_blocks(NZ, 1.0)
    yf, yi = fourier_blocks(NY, -1.0), fourier_blocks(NY, 1.0)
    xf = fourier_blocks(NX, -1.0).reshape(2, NX, 2, slabs, 2)
    xi = fourier_blocks(NX, 1.0).reshape(2, slabs, 2, 2, NX)
    return {
        "zf": table("akbj,cd->cbjadk", zf, two, shape=(4 * NZ, 4 * NZ)),
        "zi": table("akbj,cd->bcjdak", zi, two, shape=(4 * NZ, 4 * NZ)),
        "yf": table("akbj,cd->kcabjd", yf, two, shape=(4 * NY, 4 * NY)),
        "yi": table("akbj,cd->akcjdb", yi, two, shape=(4 * NY, 4 * NY)),
        "xf": table("akbst,cd->caksdtb", xf, two, shape=(4 * NX, 4 * NX)),
        "xi": table("astbk,cd->sctadbk", xi, two, shape=(4 * NX, 4 * NX)),
        "order": table(
            "ab,ef,gh->aegfbh", two, two, np.eye(NZ, dtype=np.float32), shape=(4 * NZ, 4 * NZ)
        ),
    }


def product(left, right):
    return jnp.dot(left, right, preferred_element_type=jnp.float32)


def swap_halves(values):
    return pltpu.roll(values, NZ, values.ndim - 1)


def low_half(shape):
    return lax.broadcasted_iota(jnp.int32, shape, len(shape) - 1) < NZ


def masks_of(sampling):
    pattern = sampling.astype(jnp.float32)
    other = swap_halves(pattern)
    low = low_half(pattern.shape)
    return jnp.where(low, pattern, other), jnp.where(low, other, pattern)


def coil_factors(maps):
    other = swap_halves(maps)
    low = low_half(maps.shape)
    return jnp.where(low, maps, other), jnp.where(low, -other, maps)


def first_masked(kspace, sampling, order):
    masks = masks_of(sampling)
    stacked = [
        jnp.concatenate(
            [kspace[coil][:, place * LANES : (place + 1) * LANES] for coil in (2 * pair, 2 * pair + 1)], 1
        )
        for pair in range(PAIRS)
        for place in range(2)
    ]
    ordered = product(jnp.concatenate(stacked, 0), order)
    columns = []
    for pair in range(PAIRS):
        rows = []
        for place in range(2):
            at = (2 * pair + place) * NX
            rows += [
                ordered[at : at + NX, part * LANES : (part + 1) * LANES] * masks[place]
                for part in range(2)
            ]
        columns.append(jnp.concatenate(rows, 0).astype(jnp.bfloat16))
    return jnp.concatenate(columns, 1)


def masked_spectrum(portion, sampling, xf):
    spectrum = product(xf, portion)
    columns = []
    for comp in range(sampling.shape[0]):
        masks = masks_of(sampling[comp])
        for pair in range(PAIRS):
            at = (comp * PAIRS + pair) * LANES
            rows = [
                spectrum[part * NX : (part + 1) * NX, at : at + LANES] * masks[part // 2]
                for part in range(4)
            ]
            columns.append(jnp.concatenate(rows, 0).astype(jnp.bfloat16))
    return jnp.concatenate(columns, 1)


def combine_coils(arrived, factors, yi, zi):
    rows = product(yi, arrived).astype(jnp.bfloat16)
    half = 2 * NY
    places = range(0, arrived.shape[1], LANES)
    stacked = [
        jnp.concatenate([rows[:half, at : at + LANES], rows[half:, at : at + LANES]], 1)
        for at in places
    ]
    depth = product(jnp.concatenate(stacked, 0), zi)
    images = []
    for comp in range(len(places) // PAIRS):
        straight = turned = None
        for coil in range(COILS):
            at = (comp * PAIRS + coil // 2) * half
            image = depth[at : at + half, coil % 2 * LANES : (coil % 2 + 1) * LANES]
            real_map, turn_map = factors[coil]
            straight = real_map * image if coil == 0 else straight + real_map * image
            turned = turn_map * image if coil == 0 else turned + turn_map * image
        images.append(straight + swap_halves(turned))
    return images


def spread_out(images, factors, zf, yf):
    half = 2 * NY
    stacked = []
    for image in images:
        turned = swap_halves(image)
        spread = [
            (real_map * image + turn_map * turned).astype(jnp.bfloat16)
            for real_map, turn_map in factors
        ]
        stacked += [jnp.concatenate(spread[2 * pair : 2 * pair + 2], 1) for pair in range(PAIRS)]
    depth = product(jnp.concatenate(stacked, 0), zf).astype(jnp.bfloat16)
    columns = [
        jnp.concatenate([depth[at : at + half, :LANES], depth[at : at + half, LANES:]], 0)
        for at in range(0, depth.shape[0], half)
    ]
    return product(yf, jnp.concatenate(columns, 1)).astype(jnp.bfloat16)


def row_of(one, other):
    total = None
    for at in range(0, one.shape[1], LANES):
        for row in range(0, one.shape[0], 64):
            block = (slice(row, row + 64), slice(at, at + LANES))
            term = one[block].astype(jnp.float32) * other[block].astype(jnp.float32)
            total = term if total is None else total + term
    return total.sum(0, keepdims=True)


def group_step(sums):
    totals = sums[0:2].sum(1, keepdims=True)
    bb, data = totals[0:1], totals[1:2]
    usable = jnp.logical_and(bb > 0.0, data > 0.0)
    return jnp.where(usable, 0.5 * data, 1.0) / jnp.where(usable, bb, 1.0)


def final_scales(sums):
    totals = sums.sum(1, keepdims=True)
    bb, bq, qq, mixed, square = (totals[place : place + 1] for place in range(5))
    step_one = bb / bq
    norm_next = bb - 2.0 * step_one * bq + step_one * step_one * qq
    more = 1.0 + norm_next / bb
    curve = more * more * bq + 2.0 * more * step_one * mixed + step_one * step_one * square
    step_two = norm_next / curve
    return step_one + step_two * more, step_two * step_one


def first_kernel(
    kspace_at, sampling_at, order_at, xi_at, out, sum_out, kspace, sampling, order, xi, sems
):
    copies = [pltpu.make_async_copy(order_at, order, sems.at[0])]
    copies.append(pltpu.make_async_copy(sampling_at, sampling, sems.at[1]))
    for comp in range(kspace.shape[0]):
        copies.append(pltpu.make_async_copy(kspace_at.at[comp], kspace.at[comp], sems.at[2 + comp]))
    copies.append(pltpu.make_async_copy(xi_at, xi, sems.at[2 + kspace.shape[0]]))
    for copy in copies:
        copy.start()
    copies[0].wait()
    copies[1].wait()
    columns = []
    for comp in range(kspace.shape[0]):
        copies[2 + comp].wait()
        columns.append(first_masked(kspace[comp], sampling[comp], order[...]))
    copies[-1].wait()
    masked = jnp.concatenate(columns, 1)
    out[...] = product(xi[...], masked).astype(jnp.bfloat16)
    sum_out[...] = row_of(masked, masked)


def kspace_kernel(portion, sampling, xf, xi, out, sum_out):
    masked = masked_spectrum(portion[...], sampling[...], xf[...])
    sum_out[...] = row_of(masked, masked)
    out[...] = product(xi[...], masked).astype(jnp.bfloat16)


def kspace_last_kernel(portion, sampling, xf, xi, group, here, bq, image_sums, out, sums_out):
    masked = masked_spectrum(portion[...], sampling[...], xf[...])
    out[...] = product(xi[...], masked).astype(jnp.bfloat16)
    inverse_step = 1.0 / group_step(group[...])
    qp = image_sums[1:2]
    sums_out[0:1] = here[0:1]
    sums_out[1:2] = bq[...]
    sums_out[2:3] = image_sums[0:1]
    sums_out[3:4] = (qp - bq[...]) * inverse_step
    sums_out[4:5] = (bq[...] - 2.0 * qp + row_of(masked, masked)) * (inverse_step * inverse_step)
    sums_out[5:8] = jnp.zeros((3, LANES), jnp.float32)


def image_kernel(arrived, coils, yi, zi, zf, yf, data, image_out, sums_out, out):
    factors = [coil_factors(coils[coil]) for coil in range(COILS)]
    images = combine_coils(arrived[...], factors, yi[...], zi[...])
    for comp, image in enumerate(images):
        image_out[comp] = image
    sums_out[0:1] = sum(row_of(image, image) for image in images)
    sums_out[1:2] = data[...]
    sums_out[2:8] = jnp.zeros((6, LANES), jnp.float32)
    out[...] = spread_out(images, factors, zf[...], yf[...])


def image_next_kernel(arrived, coils, yi, zi, zf, yf, b, group, image_out, sums_out, out):
    factors = [coil_factors(coils[coil]) for coil in range(COILS)]
    images = combine_coils(arrived[...], factors, yi[...], zi[...])
    for comp, image in enumerate(images):
        image_out[comp] = image
    step = group_step(group[...])
    moved = [b[comp] - step * image for comp, image in enumerate(images)]
    sums_out[0:1] = sum(row_of(image, image) for image in images)
    sums_out[1:2] = sum(row_of(image, other) for image, other in zip(images, moved))
    sums_out[2:8] = jnp.zeros((6, LANES), jnp.float32)
    out[...] = spread_out(moved, factors, zf[...], yf[...])


def last_kernel(arrived, coils, yi, zi, b, q, group, sums, coefficients, residual):
    factors = [coil_factors(coils[coil]) for coil in range(COILS)]
    images = combine_coils(arrived[...], factors, yi[...], zi[...])
    along_b, along_q = final_scales(sums[...])
    along_t = along_q / group_step(group[...])
    for comp, image in enumerate(images):
        coefficients[comp] = along_b * b[comp] - along_q * q[comp]
        residual[comp] = b[comp] - along_b * q[comp] + along_t * (q[comp] - image)


def call(body, operands, shapes, flops, space=pltpu.VMEM, scratch=(), mebibytes=32):
    held = sum(math.prod(o.shape) * o.dtype.itemsize for o in operands)
    held += sum(math.prod(s.shape) * s.dtype.itemsize for s in shapes)
    return pl.pallas_call(
        body,
        out_shape=shapes,
        in_specs=[pl.BlockSpec(memory_space=space)] * len(operands),
        out_specs=[pl.BlockSpec(memory_space=pltpu.VMEM)] * len(shapes),
        scratch_shapes=scratch,
        compiler_params=pltpu.CompilerParams(vmem_limit_bytes=mebibytes * 1024 * 1024),
        cost_estimate=pl.CostEstimate(flops=flops, bytes_accessed=held, transcendentals=0),
    )(*operands)


def exchange(values):
    return lax.all_to_all(values, "slab", split_axis=0, concat_axis=0, tiled=True)


def exclusive(axis, flips):
    return [(place, place ^ flips) for place in range(lax.axis_size(axis))]


def sum_over(values, axis, low, count):
    terms = [values]
    terms += [lax.ppermute(values, axis, exclusive(axis, flips * low)) for flips in range(1, count)]
    while len(terms) > 1:
        terms = [one + other for one, other in zip(terms[::2], terms[1::2])]
    return terms[0]


def total_of(values, steps):
    for axis, low, count in steps:
        values = sum_over(values, axis, low, count)
    return values


def shards(kspace, sensitivities, sampling):
    comps = kspace.shape[0]
    tables = {name: jnp.asarray(value) for name, value in make_tables().items()}
    coils = sensitivities.reshape(COILS, 2, NY, LANES).transpose(0, 2, 1, 3)
    coils = coils.reshape(COILS, 2 * NY, LANES)
    width = comps * PAIRS * LANES
    sent_shape = jax.ShapeDtypeStruct((4 * NX, width), jnp.bfloat16)
    image_shape = jax.ShapeDtypeStruct((comps, 2 * NY, LANES), jnp.float32)
    sum_shape = jax.ShapeDtypeStruct((1, LANES), jnp.float32)
    sums_shape = jax.ShapeDtypeStruct((8, LANES), jnp.float32)
    square = 2 * (4 * NX) * (4 * NX) * width

    def image_step(body, arrived, earlier, sums):
        operands = [arrived, coils] + [tables[name] for name in ("yi", "zi", "zf", "yf")]
        return call(body, operands + earlier, [image_shape, sums, sent_shape], 3 * square)

    first = [kspace, sampling, tables["order"], tables["xi"]]
    scratch = [pltpu.VMEM(array.shape, array.dtype) for array in first]
    scratch.append(pltpu.SemaphoreType.DMA((3 + comps,)))
    sent, data = call(first_kernel, first, [sent_shape, sum_shape], 2 * square, pltpu.HBM, scratch, 58)
    b, here, sent = image_step(image_kernel, exchange(sent), [data], sums_shape)
    arrived, group = exchange(sent), total_of(here, GROUP_STEPS[:2])
    arrived, group = lax.optimization_barrier((arrived, group))
    operands = [arrived, sampling, tables["xf"], tables["xi"]]
    sent, bq = call(kspace_kernel, operands, [sent_shape, sum_shape], 2 * square)
    sent, group = lax.optimization_barrier((sent, group))
    group = total_of(group, GROUP_STEPS[2:])
    q, image_sums, sent = image_step(image_next_kernel, exchange(sent), [b, group], sums_shape)
    operands = [exchange(sent), sampling, tables["xf"], tables["xi"], group, here, bq, image_sums]
    sent, sums = call(kspace_last_kernel, operands, [sent_shape, sums_shape], 2 * square)
    arrived = exchange(sent)
    operands = [arrived, coils, tables["yi"], tables["zi"], b, q, group, total_of(sums, STEPS)]
    outputs = call(last_kernel, operands, [image_shape] * 2, 2 * square)
    return tuple(
        output.reshape(comps, NY, 2, LANES).transpose(0, 2, 1, 3).reshape(comps, 2, -1)
        for output in outputs
    )


def solution(mesh):
    in_specs = (P("comp", None, None, "slab"), P(None, "slab", None), P("comp", None, "slab"))
    out_specs = (P("comp", "slab", None), P("comp", "slab", None))
    return jax.shard_map(shards, mesh=mesh, in_specs=in_specs, out_specs=out_specs, check_vma=False)
```
